256 devices in a mesh: space: 64 (over x_hi, y, z), tm: 4 (over x_lo, core).
Axes of the slice: x: 4 (x_hi: 2, x_lo: 2; x = x_hi * 2 + x_lo), y: 4, z: 8, core: 2. Of those that a mesh axis runs over, the one named last changes fastest.
Arguments:
- field: float32 [10, 16, 256, 128, 128], P(None, 'tm', 'space'), may hold values from -6 to 6
Outputs:
- spectrum: float32 [2, 10, 16, 1024, 32], P(None, None, 'tm', 'space')
The draws below stay inside these ranges and needn't reach their ends.
All inputs are finite; a program needn't handle non-finite values.
Results may differ from the reference program's by a relative error of at most 0.00007.
Values sent between devices are 32-bit elements; how exact they have to be, the bound alone decides.
A program may use at most 128 MiB of HBM per device.

```python
import math
import jax
import jax.numpy as jnp
from jax import lax

CH = 10
NX = 128
NY = 128
NT = 16
MX = 32
MY = 32
MZ = 32
KT = 16
NZ = 256


def block_levels(stream_key, dims, cuts, low, largest):
    factor_of, own = 1.0, jax.random.fold_in(stream_key, 6)
    for dim, parts in cuts:
        steps = jnp.exp(jax.random.uniform(jax.random.fold_in(own, dim), (parts,), jnp.float32, low / len(cuts), largest / len(cuts)))
        factor_of = factor_of * jnp.repeat(steps, dims[dim] // parts).reshape([-1 if axis == dim else 1 for axis in range(len(dims))])
    return factor_of


def noise(rng, extent, width, limit, shards=(), kind=jnp.bfloat16):
    drawn = width * jax.random.normal(rng, extent, jnp.float32)
    if shards:
        drawn = drawn * block_levels(rng, extent, shards, -0.22, 0.18)
    return jnp.clip(drawn, -limit, limit).astype(kind)


def setup_inputs(seed: int = 0) -> dict:
    arg_keys = jax.random.split(jax.random.key(seed), 2)
    return {
        "field": noise(arg_keys[0], (CH, NT, NZ, NX, NY), 1.0, 6.0, ((1, 4), (2, 64)), jnp.float32),
    }


def signed_freq(count):
    index = jnp.arange(count, dtype=jnp.int32)
    return jnp.where(index < count // 2, index, index - count)

def table(freq, positions, length):
    product = jnp.mod(freq[:, None] * positions[None, :], length)
    angle = 2.0 * math.pi / length * product.astype(jnp.float32)
    return jnp.stack([jnp.cos(angle), -jnp.sin(angle)])

def cmix(weights, data, form):
    hp = lax.Precision.HIGHEST
    real_part = jnp.einsum(form, weights[0], data[0], precision=hp) - jnp.einsum(form, weights[1], data[1], precision=hp)
    imag_part = jnp.einsum(form, weights[1], data[0], precision=hp) + jnp.einsum(form, weights[0], data[1], precision=hp)
    return jnp.stack([real_part, imag_part])

def reference(field):
    w_y = table(signed_freq(MY), jnp.arange(NY, dtype=jnp.int32), NY)
    w_x = table(signed_freq(MX), jnp.arange(NX, dtype=jnp.int32), NX)
    w_z = table(jnp.arange(MZ, dtype=jnp.int32), jnp.arange(NZ, dtype=jnp.int32), NZ)
    w_t = table(signed_freq(KT), jnp.arange(NT, dtype=jnp.int32), NT)

    def spatial(plane):
        along_y = jnp.einsum('cby,zxy->czxb', w_y, plane, precision=lax.Precision.HIGHEST)
        along_x = cmix(w_x, along_y, 'ax,zxb->zba')
        return cmix(w_z, along_x, 'kz,zba->bak')
    flat = field.reshape(CH * NT, NZ, NX, NY)
    per_step = lax.map(spatial, flat)
    per_step = per_step.reshape(CH, NT, 2, MY, MX, MZ)
    per_step = jnp.transpose(per_step, (2, 0, 1, 3, 4, 5))
    scale = 1.0 / math.sqrt(NX * NY * NZ * NT)
    result = cmix(w_t, per_step, 'qt,ntbak->nqbak') * scale
    return result.reshape(2, CH, KT, MY * MX, MZ)
```

```python
import functools
import math

import jax
import jax.numpy as jnp
import ml_dtypes
import numpy as np
from jax import lax
from jax.experimental import pallas as pl
from jax.experimental.pallas import tpu as pltpu
from jax.sharding import PartitionSpec as P

MESH = pl.DeviceIdType.MESH
BF = jnp.bfloat16
F32 = jnp.float32

CH = 10
NX = 128
NY = 128
NT = 16
NZ = 256
SPACE = 64
TM = 4
GROUPS = ((0, 4), (4, 4), (8, 2))
STEP = 24
MOVES = ((0, 1), (1, 3))
OFFSETS = sorted(
    [(k // 32, (k // 8) % 4, k % 8) for k in range(1, SPACE)],
    key=lambda at: (-2 * at[0] - min(at[1], 4 - at[1]) - min(at[2], 8 - at[2]), at[1], at[2]),
)
PLANE_OFFSETS = [(1, 2), (1, 1), (1, 3), (1, 0), (0, 2), (0, 1), (0, 3), (0, 0)]
TIME_AT = (0, 32, 64, 80)


def halves(table):
    high = table.astype(ml_dtypes.bfloat16)
    low = (table - high.astype(np.float64)).astype(ml_dtypes.bfloat16)
    return high, low


def angle(freq, pos, length):
    return 2.0 * math.pi * ((freq * pos) % length) / length


def real_modes(order):
    cells = np.arange(128)
    rows = np.zeros((40, 128))
    for e in range(16):
        rows[order(e, 0)] = np.cos(angle(e, cells, 128))
        rows[order(e, 1)] = np.sin(angle(e, cells, 128)) if e else np.cos(angle(16, cells, 128))
    rows[32] = np.sin(angle(16, cells, 128))
    return rows


def plane_tables():
    def build(order):
        high, low = halves(real_modes(order))
        return np.concatenate([np.concatenate([high, high], 1), np.concatenate([low, low], 1)], 0)

    wx = build(lambda e, c: 2 * e + c)
    up = build(lambda e, c: 16 * c + e)
    down = build(lambda e, c: 16 * c + (16 - e) % 16)
    return wx, np.stack([up, down])


def depth_tables():
    depth = np.arange(NZ)
    k = np.arange(32)[:, None]
    both = np.concatenate([np.cos(angle(k, depth, NZ)), np.sin(angle(k, depth, NZ))], 0)
    main = np.zeros((2, 64, SPACE, 2, 4))
    for c in range(2):
        main[c, :, :, c, :] = both.reshape(64, SPACE, 4)
    main = main.reshape(128, 512)
    main2 = main.reshape(-1, SPACE, 2, 2, 2).transpose(0, 3, 1, 2, 4).reshape(-1, 512)
    both2 = both.reshape(-1, SPACE, 2, 2).transpose(0, 2, 1, 3).reshape(-1, 256)
    return [np.concatenate(halves(table), 0) for table in (main, main2, both, both2)]


def time_tables():
    def phase(q, step):
        return np.exp(-1j * angle(q if q < 8 else q - 16, step, NT))

    def pack(table, pad):
        high, low = halves(table)
        blank = np.zeros(table.shape[:-1] + (pad,), ml_dtypes.bfloat16)
        return np.concatenate([np.concatenate([part, part, blank], -1) for part in (high, low)], -2)

    out = []
    for count in (4, 2):
        table = np.zeros((2, 2, 2, 2, TM, 8, TM, 2, count, 4))
        for n in range(count):
            half, rest = divmod(n, count // 2)
            for q in range(16):
                for step in range(16):
                    value = phase(q, step)
                    for sx, sign in ((0, 1), (1, -1)):
                        at = (sx, q // 4, (q % 4) * 2 + rest, step // 4)
                        for zero in range(2):
                            if zero:
                                terms = ((sx, value),)
                            else:
                                terms = ((0, value), (1, -1j * sign * value))
                            for c, term in terms:
                                table[(zero, half, 0) + at + (c, n, step % 4)] = term.real
                                table[(zero, half, 1) + at + (c, n, step % 4)] = term.imag
        out.append(pack(table.reshape(2, 256, 32 * count), 0))
    table = np.zeros((3, 2, 2, TM, 8, TM, CH, 4))
    for n in range(CH):
        ng = n // 4
        half, rest = divmod(n % 4, 2) if ng < 2 else (n - 8, 0)
        for q in range(16):
            for step in range(16):
                term = 1j * phase(q, step)
                at = (q // 4, (q % 4) * 2 + rest, step // 4, n, step % 4)
                table[(ng, half, 0) + at] = term.real
                table[(ng, half, 1) + at] = term.imag
    out.append(pack(table.reshape(384, 160), 64))
    return out


def lane_tables():
    scale = 1.0 / math.sqrt(NX * NY * NZ * NT)
    out = np.zeros((3, 2, 2, 128, 2, 2, 2, 32))
    for sy, sign in ((0, 1), (1, -1)):
        for k in range(32):
            for kind in range(3):
                coef = np.zeros(128, complex)
                if kind == 0:
                    coef[k], coef[32 + k] = 1, -1j
                    coef[64 + k], coef[96 + k] = -1j * sign, -sign
                elif kind == 1:
                    at = 64 * sy
                    coef[at + k], coef[at + 32 + k] = 1, -1j
                elif sy == 1:
                    coef[k], coef[32 + k] = 1j, 1
                for w in range(2):
                    out[kind, w, 0, :, sy, w, 0, k] = coef.real
                    out[kind, w, 1, :, sy, w, 0, k] = -coef.imag
                    out[kind, w, 0, :, sy, w, 1, k] = coef.imag
                    out[kind, w, 1, :, sy, w, 1, k] = coef.real
    return (out.reshape(3, 512, 256) * scale).astype(ml_dtypes.bfloat16)


def all_tables():
    wx, wy = plane_tables()
    wz, wz2, wzb, wzb2 = depth_tables()
    m01, m2, mx = time_tables()
    pieces = {
        "wx": wx, "wy": wy.reshape(160, 256), "m01": m01.reshape(1024, 256), "m2": np.concatenate([m2[0], m2[1]], 1),
        "lanes": lane_tables().reshape(1536, 256), "wzb": wzb, "wzb2": wzb2,
    }
    for name, table in (("wz", wz), ("wz2", wz2), ("mx", mx)):
        wide = np.concatenate([table, np.zeros((len(table), -table.shape[1] % 256), ml_dtypes.bfloat16)], 1)
        pieces[name] = np.concatenate([wide[:, :256], wide[:, 256:]], 0)
    first, at = {}, 0
    for name, table in pieces.items():
        first[name] = at
        at += len(table)
    return np.concatenate(list(pieces.values()), 0), first


def split(values):
    high = values.astype(BF)
    return high, (values - high.astype(F32)).astype(BF)


def dot(a, b):
    return jnp.dot(a, b, preferred_element_type=F32)


def owner(g, u):
    return jnp.where(u < 2, 2 * g + u, jnp.where(g == 0, 32, 64 - 2 * g) + u - 2)


def place(s):
    b, h = s // 2, s % 2
    g = jnp.where(b < 16, b, jnp.where(b == 16, 0, 32 - b))
    return g, jnp.where(b < 16, h, 2 + h)


def kernel(
    at_of, field, tables, out,
    planes, rows, rows_x, wx, wy, wz, wz2, wzb, wzb2, m01, m2, mx, lanes, lanes_b,
    send_a, send_b, recv_a, recv_b, time_send, time_send_x, time_sb, time_sbx,
    time_recv, time_recv_x, time_rb, time_rbx, sorts, last, blocks,
    field_sem, const_sem, ssa, rsa, ssx, rsx, ssb, rsb, sst, rst, sstx, rstx, sstb, rstb, sstbx, rstbx, ssl, rsl,
):
    s, tm = lax.axis_index("space"), lax.axis_index("tm")
    g, u = place(s)
    e = 4 * u + tm
    zero_g, zero_e, zero_u = g == 0, e == 0, u == 0
    pick_e, pick_g = jnp.where(zero_e, 1, 0), jnp.where(zero_g, 1, 0)

    def field_copy(pair):
        two = pl.ds(2 * pair, 2)
        return pltpu.make_async_copy(field.at[two], planes.at[two], field_sem.at[pair])

    def table_copy(i, dst, name, skip=0, columns=slice(None)):
        rows_at = pl.ds(pl.multiple_of(at_of[name] + skip, 16), dst.shape[0])
        return pltpu.make_async_copy(tables.at[rows_at, columns], dst, const_sem.at[i])

    consts = [
        table_copy(0, wx, "wx"),
        table_copy(1, wy, "wy"),
        table_copy(2, wz.at[:, :256], "wz"),
        table_copy(3, wz.at[:, 256:], "wz", 256),
        table_copy(4, wzb, "wzb"),
        table_copy(5, wzb2, "wzb2"),
        table_copy(6, m01, "m01", 512 * pick_e),
        table_copy(7, m2, "m2", 0, pl.ds(pl.multiple_of(128 * pick_e, 128), 128)),
        table_copy(8, mx.at[:, :256], "mx"),
        table_copy(9, mx.at[:, 256:], "mx", 768, slice(0, 128)),
        table_copy(10, lanes, "lanes", 512 * pick_g),
        table_copy(11, lanes_b, "lanes", 1024),
        table_copy(12, wz2.at[:, :256], "wz2"),
        table_copy(13, wz2.at[:, 256:], "wz2", 256),
    ]
    consts[0].start()
    field_copy(0).start()
    consts[1].start()

    barrier = pltpu.get_barrier_semaphore()

    def greet(space, time):
        pl.semaphore_signal(barrier, inc=1, device_id={"space": space, "tm": time}, device_id_type=MESH)


    def turn(value, count):
        return jnp.where(value >= count, value - count, value)

    place_x, place_y, place_z = s // 32, (s // 8) % 4, s % 8
    along = (
        [32 * turn(place_x + d, 2) for d in range(2)],
        [8 * turn(place_y + d, 4) for d in range(4)],
        [turn(place_z + d, 8) for d in range(8)],
    )
    round_z = turn(place_z, 6)
    z_order = [turn(turn(round_z + i, 6) + 6, 8) for i in range(6)] + [4 + turn(place_z % 2 + i, 2) for i in range(2)]
    others = [along[0][x] + along[1][y] + along[2][z] for x, y, z in OFFSETS]
    for to in others:
        greet(to, tm)

    for j in range(1, TM):
        greet(s, turn(tm + j, TM))
        for v in range(1, 4):
            greet(owner(g, turn(u + v, 4)), turn(tm + j, TM))

    for pair in range(1, CH // 2):
        field_copy(pair).start()
    for copy in consts[2:]:
        copy.start()

    rows_x[...] = jnp.zeros_like(rows_x)
    send_b[...] = jnp.zeros_like(send_b)

    def plane_step(ng, first, n):
        products = []
        for t in range(4):
            for pair in range(2):
                high, low = split(jnp.concatenate([planes[n, t, 2 * pair], planes[n, t, 2 * pair + 1]], axis=1))
                both = dot(wx[...], jnp.concatenate([high, low], axis=0))
                products.append((t, pair, both[:40] + both[40:]))
        for t, pair, both in products:
            at = pl.multiple_of(((n - first) * 4 + t) * 8, 8)
            for half in range(2):
                z = 2 * pair + half
                part = both[:, 128 * half : 128 * half + 128]
                for v in range(4):
                    tile = part[8 * v : 8 * v + 8]
                    if ng < 2:
                        rows[ng, z, pl.ds(v * 128 + at, 8), :] = tile
                    else:
                        rows[2, half, pl.ds(v * 128 + pair * 64 + at, 8), :] = tile
                rows_x[half, pl.ds(64 * pair + 4 * n + t, 1), :] = part[32:33]

    def along_y(values, side):
        high, low = split(values)
        both = lax.dot_general(
            wy[80 * side : 80 * side + 80, :], jnp.concatenate([high, low], axis=1), (((1,), (1,)), ((), ())),
            preferred_element_type=F32,
        )
        return both[:40] + both[40:]

    def exchange(ng):
        count = 4 if ng < 2 else 2
        products = [
            (z, side, along_y(rows[ng, z, 256 * side : 256 * side + 256, :], side)) for z in range(count) for side in range(2)
        ]
        extras = [along_y(rows_x[z], 0) for z in range(2)] if ng == 2 else []
        for z, side, both in products:
            for h in range(2):
                lanes_h = slice(128 * h, 128 * h + 128)
                for c in range(2):
                    at = (side * 32 + h) * STEP + 8 * ng + count * c + z
                    send_a[pl.ds(at, 16, stride=2 * STEP), :] = both[16 * c : 16 * c + 16, lanes_h]
                send_b[pl.ds((2 * side + h) * 12 + 4 * ng + z, 1), :] = both[32:33, lanes_h]
        for z, both in enumerate(extras):
            for c in range(2):
                send_a[pl.ds(20 + 2 * c + z, 16, stride=2 * STEP), :] = both[16 * c : 16 * c + 16]
            send_b[pl.ds(10 + z, 1), :] = both[32:33]

    def sent(move):
        first, end = MOVES[move]
        return 8 * first, 8 * (end - first) - (4 if end == 3 else 0)

    def sent_b(move):
        first, end = MOVES[move]
        return 4 * first, 4 * (end - first)

    def remote(src, dst, send_sem, recv_sem, space, time):
        return pltpu.make_async_remote_copy(
            src_ref=src, dst_ref=dst, send_sem=send_sem, recv_sem=recv_sem,
            device_id={"space": space, "tm": time}, device_id_type=MESH,
        )

    def space_copy(move, to):
        first, count = sent(move)
        src = pl.ds(pl.multiple_of(to * STEP + first, 8), count)
        return remote(send_a.at[src], recv_a.at[s, pl.ds(first, count)], ssa.at[move], rsa.at[move], to, tm)

    def send_space(move):
        first, count = sent(move)
        here = (s, pl.ds(first, count))
        last_move = move == len(MOVES) - 1

        for z in z_order:
            for x, y in PLANE_OFFSETS:
                to = along[0][x] + along[1][y] + z
                if x or y:
                    space_copy(move, to).start()
                else:
                    @pl.when(to != s)
                    def _():
                        space_copy(move, to).start()

        if last_move:
            here_x = (s, pl.ds(20, 4))

            @pl.loop(0, 16)
            def _(k):
                @pl.when(2 * k != s)
                def _():
                    src = pl.ds(pl.multiple_of(2 * k * STEP + 20, 4), 4)
                    remote(send_a.at[src], recv_a.at[here_x], ssx.at[0], rsx.at[0], 2 * k, tm).start()

            @pl.when(zero_u)
            def _():
                recv_a[here_x] = send_a[pl.ds(pl.multiple_of(s * STEP + 20, 4), 4), :]

        first_b, count_b = sent_b(move)
        here_b = (s, pl.ds(first_b, count_b))
        for v, to in enumerate((0, 1, 32, 33)):
            src = pl.ds(12 * v + first_b, count_b)

            @pl.when(s != to)
            def _():
                remote(send_b.at[src], recv_b.at[here_b], ssb.at[move], rsb.at[move], to, tm).start()

            @pl.when(s == to)
            def _():
                recv_b[here_b] = send_b[src, :]

        recv_a[here] = send_a[pl.ds(pl.multiple_of(s * STEP + first, 8), count), :]

    consts[0].wait()
    for ng, (first, count) in enumerate(GROUPS):
        @pl.loop(first, first + count, step=2)
        def _(n):
            field_copy(n // 2).wait()
            plane_step(ng, first, n)
            plane_step(ng, first, n + 1)

        if ng == 0:
            consts[1].wait()
        exchange(ng)
        if ng == 0:
            pl.semaphore_wait(barrier, 63 + 3 + 9)
        for move, (_, end) in enumerate(MOVES):
            if ng == end - 1:
                send_space(move)

    for copy in consts[2:]:
        copy.wait()

    def wait_rows(rows_of, count, sem):
        pltpu.make_async_copy(rows_of.at[pl.ds(0, count)], rows_of.at[pl.ds(0, count)], sem).wait()

    def moved(ng):
        return TIME_AT[ng], TIME_AT[ng + 1] - TIME_AT[ng]

    def keep_time(ng, sort, z_rows, src, src_x):
        count = (TIME_AT[ng + 1] - TIME_AT[ng]) // 2
        sort[...] = z_rows
        for v in range(TM):
            for c in range(2):
                at = 80 * v + TIME_AT[ng] + count * c
                src[at : at + count, :] = sort[pl.ds(2 * v + c, count, stride=8), :]
        if ng == 2:
            src_x[...] = z_rows[64:104]

    def send_time(ng, src, src_x, dst, dst_x, send_sem, recv_sem, send_sem_x, recv_sem_x):
        first, count = moved(ng)
        mine = pl.ds(pl.multiple_of(tm * 80 + first, 8), count)
        here = (tm, pl.ds(first, count))
        for j in range(1, TM):
            to = tm + j
            to = jnp.where(to >= TM, to - TM, to)
            there = pl.ds(pl.multiple_of(to * 80 + first, 8), count)
            remote(src.at[there], dst.at[here], send_sem.at[ng], recv_sem.at[ng], s, to).start()
        dst[here] = src[mine, :]
        if ng == 2:
            at_x = pl.ds(pl.multiple_of(tm * 40, 8), 40)

            @pl.when(jnp.logical_and(zero_u, tm != 0))
            def _():
                remote(src_x, dst_x.at[at_x], send_sem_x.at[0], recv_sem_x.at[0], s, 0).start()

            @pl.when(zero_e)
            def _():
                dst_x[pl.ds(0, 40), :] = src_x[...]

    time_a = (time_send, time_send_x, time_recv, time_recv_x, sst, rst, sstx, rstx)
    time_b = (time_sb, time_sbx, time_rb, time_rbx, sstb, rstb, sstbx, rstbx)

    def received(ref, ng):
        size = ref.shape[1] // 3
        count = SPACE * size
        values = ref[:, size * ng : size * ng + size, :].reshape(count, 128) if ng < 2 else None
        if ng == 2:
            count //= 2
            main, extra = (
                ref[:, at : at + size // 2, :].reshape(count, 128) for at in (2 * size, 2 * size + size // 2)
            )
            lower = lax.broadcasted_iota(jnp.int32, (count, 128), 1) < 64
            values = jnp.concatenate(
                [jnp.where(lower, main, pltpu.roll(extra, 64, 1)), jnp.where(lower, pltpu.roll(main, 64, 1), extra)], axis=0
            )
        high, low = split(values)
        return jnp.concatenate([high, low], axis=1)

    def depth_step(move):
        first, end = MOVES[move]
        wait_rows(send_a, 63 * sent(move)[1], rsa.at[move])
        if end == 3:
            @pl.when(zero_u)
            def _():
                wait_rows(send_a, 63 * 4, rsx.at[0])

        for ng in range(first, end):
            both = dot(wz[...] if ng < 2 else wz2[...], received(recv_a, ng))
            keep_time(ng, sorts.at[ng], (both[:128, :128] + both[:128, 128:] + both[128:, :128]).T, *time_a[:2])
            send_time(ng, *time_a)

        @pl.when(zero_g)
        def _():
            wait_rows(send_a, 63 * sent_b(move)[1], rsb.at[move])
            for ng in range(first, end):
                both = dot(wzb[...] if ng < 2 else wzb2[...], received(recv_b, ng))
                z_rows = both[:64, :128] + both[:64, 128:] + both[64:, :128]
                keep_time(ng, sorts.at[3 + ng], jnp.concatenate([z_rows, jnp.zeros_like(z_rows)], axis=0).T, *time_b[:2])
                send_time(ng, *time_b)

    def finish(values, table, signs):
        high, low = split(values)
        fill = table.shape[1] - 2 * values.shape[0]
        parts = [high, low] + ([jnp.zeros((fill, 128), BF)] if fill else [])
        both = dot(table[...], jnp.concatenate(parts, axis=0))
        both = both[: both.shape[0] // 2] + both[both.shape[0] // 2 :]
        count = both.shape[0] // 4
        pairs = [split(both[count * i : count * i + count]) for i in range(4)]
        both = jnp.concatenate([jnp.concatenate([pair[i] for pair in pairs], axis=1) for i in range(2)], axis=0)
        both = dot(both, signs[...])
        return both[:count] + both[count:]

    def keep(ng, value, first, add):
        for i in range(value.shape[0] // 8):
            for sy in range(2):
                j = 8 * sy + first + i
                part = value[8 * i : 8 * i + 8, 128 * sy : 128 * sy + 128]
                at = slice(j * STEP + 8 * ng, j * STEP + 8 * ng + 8)
                last[at, :] = last[at, :] + part if add else part

    def slot_of(sx):
        return jnp.where(sx == 0, e, jnp.where(zero_e, 0, 16 - e))

    def last_copy(j, first, count):
        at = pl.ds(pl.multiple_of(slot_of((j // 4) % 2) * STEP + first, 8), count)
        src = pl.ds(pl.multiple_of(j * STEP + first, 8), count)
        return remote(last.at[src], blocks.at[at], ssl.at[0], rsl.at[0], owner(g, j // 4), j % 4)

    def steps_of(ref, ng):
        count = TIME_AT[ng + 1] - TIME_AT[ng]
        return ref[:, TIME_AT[ng] : TIME_AT[ng + 1], :].reshape(TM * count, 128)

    def time_step(ng):
        table = m01 if ng < 2 else m2
        wait_rows(time_send, 3 * moved(ng)[1], rst.at[ng])
        keep(ng, finish(steps_of(time_recv, ng), table, lanes), 0, False)
        if ng == 2:
            @pl.when(zero_e)
            def _():
                wait_rows(time_recv_x, 120, rstx.at[0])
                value = finish_x(time_recv_x, lanes)
                for i in range(3):
                    keep(i, value[32 * i : 32 * i + 32], 4, True)

        @pl.when(zero_g)
        def _():
            wait_rows(time_sb, 3 * moved(ng)[1], rstb.at[ng])
            keep(ng, finish(steps_of(time_rb, ng), table, lanes_b), 0, True)
            if ng == 2:
                @pl.when(zero_e)
                def _():
                    wait_rows(time_rbx, 120, rstbx.at[0])
                    value = finish_x(time_rbx, lanes_b)
                    for i in range(3):
                        keep(i, value[32 * i : 32 * i + 32], 4, True)

        @pl.when(jnp.logical_not(zero_e))
        def _():
            side = jnp.where(e >= 8, 8, 0)
            for k in range(8):
                last_copy(8 - side + k, 8 * ng, 8).start()
            for k in range(1, 8):
                last_copy(side + turn(e - side + k, 8), 8 * ng, 8).start()

        @pl.when(zero_e)
        def _():
            for j in (8, 9, 10, 11, 1, 2, 3):
                last_copy(j, 8 * ng, 8).start()
            if ng == 2:
                for j in (12, 13, 14, 15, 4, 5, 6, 7):
                    last_copy(j, 0, STEP).start()

        at = pl.ds(pl.multiple_of(slot_of(u % 2) * STEP + 8 * ng, 8), 8)
        blocks[at, :] = last[pl.ds(pl.multiple_of(e * STEP + 8 * ng, 8), 8), :]

    def finish_x(ref, signs):
        high, low = split(ref[...])
        both = dot(mx[...], jnp.concatenate([high, low, jnp.zeros((64, 128), BF)], axis=0))
        both = both[:384] + both[384:]
        values = []
        for i in range(3):
            pairs = [split(both[128 * i + 32 * j : 128 * i + 32 * j + 32]) for j in range(4)]
            value = jnp.concatenate([jnp.concatenate([pair[h] for pair in pairs], axis=1) for h in range(2)], axis=0)
            value = dot(value, signs[...])
            values.append(value[:32] + value[32:])
        return jnp.concatenate(values, axis=0)

    for move, groups in enumerate(MOVES):
        depth_step(move)
        for ng in range(*groups):
            time_step(ng)

    wait_rows(blocks, 15 * STEP, rsl.at[0])
    for ng in range(3):
        for r in range(8):
            q, rest = r // 2, r % 2
            if ng == 2 and rest:
                continue
            value = blocks[pl.ds(8 * ng + r, 16, stride=STEP), :]
            for half in range(2):
                n = 4 * ng + 2 * half + rest if ng < 2 else 8 + half
                for part in range(2):
                    at = 64 * half + 32 * part
                    out[part, n, q] = value[:, at : at + 32]

    wait_rows(blocks, 15 * STEP, ssl.at[0])
    for move, (first, end) in enumerate(MOVES):
        wait_rows(send_a, 63 * sent(move)[1], ssa.at[move])

        @pl.when(zero_g)
        def _():
            wait_rows(send_b, 3 * sent_b(move)[1], ssb.at[move])

        @pl.when(jnp.logical_not(zero_g))
        def _():
            wait_rows(send_b, 4 * sent_b(move)[1], ssb.at[move])

    for ng in range(3):
        wait_rows(time_send, 3 * moved(ng)[1], sst.at[ng])

        @pl.when(zero_g)
        def _():
            wait_rows(time_sb, 3 * moved(ng)[1], sstb.at[ng])

    @pl.when(zero_u)
    def _():
        wait_rows(send_a, 15 * 4, ssx.at[0])

    @pl.when(jnp.logical_not(zero_u))
    def _():
        wait_rows(send_a, 16 * 4, ssx.at[0])

    @pl.when(jnp.logical_and(zero_u, tm != 0))
    def _():
        wait_rows(time_send_x, 40, sstx.at[0])

        @pl.when(zero_g)
        def _():
            wait_rows(time_sbx, 40, sstbx.at[0])


def body(field):
    tables, at_of = all_tables()
    dma = pltpu.SemaphoreType.DMA

    def vmem(*shape):
        return pltpu.VMEM(shape, F32)

    def table(*shape):
        return pltpu.VMEM(shape, BF)

    return pl.pallas_call(
        functools.partial(kernel, at_of),
        out_shape=jax.ShapeDtypeStruct((2, CH, 4, 16, 32), F32),
        in_specs=[pl.BlockSpec(memory_space=pltpu.HBM)] * 2,
        out_specs=pl.BlockSpec(memory_space=pltpu.VMEM),
        scratch_shapes=[
            vmem(CH, 4, 4, 128, 128),
            vmem(3, 4, 512, 128), vmem(2, 128, 128),
            table(80, 256), table(160, 256), table(256, 512), table(256, 512), table(128, 256), table(128, 256),
            table(512, 256), table(512, 128), table(768, 384),
            table(512, 256), table(512, 256),
            vmem(64 * STEP, 128), vmem(48, 128), vmem(64, STEP, 128), vmem(64, 12, 128),
            vmem(320, 128), vmem(40, 128), vmem(320, 128), vmem(40, 128),
            vmem(4, 80, 128), vmem(160, 128), vmem(4, 80, 128), vmem(160, 128),
            vmem(6, 128, 128), vmem(16 * STEP, 128), vmem(16 * STEP, 128),
            dma((CH // 2,)), dma((14,)),
            dma((len(MOVES),)), dma((len(MOVES),)), dma((1,)), dma((1,)), dma((len(MOVES),)), dma((len(MOVES),)),
            dma((3,)), dma((3,)), dma((1,)), dma((1,)), dma((3,)), dma((3,)), dma((1,)), dma((1,)),
            dma((1,)), dma((1,)),
        ],
        compiler_params=pltpu.CompilerParams(
            collective_id=0, has_side_effects=True, vmem_limit_bytes=52 * 1024 * 1024
        ),
        cost_estimate=pl.CostEstimate(flops=20_000_000_000, bytes_accessed=13_000_000, transcendentals=0),
    )(field, tables)


def solution(mesh):
    return jax.shard_map(
        body,
        mesh=mesh,
        in_specs=(P(None, "tm", "space", None, None),),
        out_specs=P(None, None, "tm", "space", None),
        check_vma=False,
    )
```

```python
import functools
import math

import jax
import jax.numpy as jnp
import ml_dtypes
import numpy as np
from jax import lax
from jax.experimental import pallas as pl
from jax.experimental.pallas import tpu as pltpu
from jax.sharding import PartitionSpec as P

MESH = pl.DeviceIdType.MESH
BF = jnp.bfloat16
F32 = jnp.float32

CH = 10
NX = 128
NY = 128
NT = 16
NZ = 256
SPACE = 64
TM = 4
GROUPS = ((0, 4), (4, 4), (8, 2))
STEP = 24
MOVES = ((0, 1), (1, 3))
OFFSETS = sorted(
    [(k // 32, (k // 8) % 4, k % 8) for k in range(1, SPACE)],
    key=lambda at: (-2 * at[0] - min(at[1], 4 - at[1]) - min(at[2], 8 - at[2]), at[1], at[2]),
)
TIME_AT = (0, 32, 64, 80)


def halves(table):
    high = table.astype(ml_dtypes.bfloat16)
    low = (table - high.astype(np.float64)).astype(ml_dtypes.bfloat16)
    return high, low


def angle(freq, pos, length):
    return 2.0 * math.pi * ((freq * pos) % length) / length


def real_modes(order):
    cells = np.arange(128)
    rows = np.zeros((40, 128))
    for e in range(16):
        rows[order(e, 0)] = np.cos(angle(e, cells, 128))
        rows[order(e, 1)] = np.sin(angle(e, cells, 128)) if e else np.cos(angle(16, cells, 128))
    rows[32] = np.sin(angle(16, cells, 128))
    return rows


def plane_tables():
    def build(order):
        high, low = halves(real_modes(order))
        return np.concatenate([np.concatenate([high, high], 1), np.concatenate([low, low], 1)], 0)

    wx = build(lambda e, c: 2 * e + c)
    up = build(lambda e, c: 16 * c + e)
    down = build(lambda e, c: 16 * c + (16 - e) % 16)
    return wx, np.stack([up, down])


def depth_tables():
    depth = np.arange(NZ)
    k = np.arange(32)[:, None]
    both = np.concatenate([np.cos(angle(k, depth, NZ)), np.sin(angle(k, depth, NZ))], 0)
    main = np.zeros((2, 64, SPACE, 2, 4))
    for c in range(2):
        main[c, :, :, c, :] = both.reshape(64, SPACE, 4)
    main = main.reshape(128, 512)
    main2 = main.reshape(-1, SPACE, 2, 2, 2).transpose(0, 3, 1, 2, 4).reshape(-1, 512)
    both2 = both.reshape(-1, SPACE, 2, 2).transpose(0, 2, 1, 3).reshape(-1, 256)
    return [np.concatenate(halves(table), 0) for table in (main, main2, both, both2)]


def time_tables():
    def phase(q, step):
        return np.exp(-1j * angle(q if q < 8 else q - 16, step, NT))

    def pack(table, pad):
        high, low = halves(table)
        blank = np.zeros(table.shape[:-1] + (pad,), ml_dtypes.bfloat16)
        return np.concatenate([np.concatenate([part, part, blank], -1) for part in (high, low)], -2)

    out = []
    for count in (4, 2):
        table = np.zeros((2, 2, 2, 2, TM, 8, TM, 2, count, 4))
        for n in range(count):
            half, rest = divmod(n, count // 2)
            for q in range(16):
                for step in range(16):
                    value = phase(q, step)
                    for sx, sign in ((0, 1), (1, -1)):
                        at = (sx, q // 4, (q % 4) * 2 + rest, step // 4)
                        for zero in range(2):
                            if zero:
                                terms = ((sx, value),)
                            else:
                                terms = ((0, value), (1, -1j * sign * value))
                            for c, term in terms:
                                table[(zero, half, 0) + at + (c, n, step % 4)] = term.real
                                table[(zero, half, 1) + at + (c, n, step % 4)] = term.imag
        out.append(pack(table.reshape(2, 256, 32 * count), 0))
    table = np.zeros((3, 2, 2, TM, 8, TM, CH, 4))
    for n in range(CH):
        ng = n // 4
        half, rest = divmod(n % 4, 2) if ng < 2 else (n - 8, 0)
        for q in range(16):
            for step in range(16):
                term = 1j * phase(q, step)
                at = (q // 4, (q % 4) * 2 + rest, step // 4, n, step % 4)
                table[(ng, half, 0) + at] = term.real
                table[(ng, half, 1) + at] = term.imag
    out.append(pack(table.reshape(384, 160), 64))
    return out


def lane_tables():
    scale = 1.0 / math.sqrt(NX * NY * NZ * NT)
    out = np.zeros((3, 2, 2, 128, 2, 2, 2, 32))
    for sy, sign in ((0, 1), (1, -1)):
        for k in range(32):
            for kind in range(3):
                coef = np.zeros(128, complex)
                if kind == 0:
                    coef[k], coef[32 + k] = 1, -1j
                    coef[64 + k], coef[96 + k] = -1j * sign, -sign
                elif kind == 1:
                    at = 64 * sy
                    coef[at + k], coef[at + 32 + k] = 1, -1j
                elif sy == 1:
                    coef[k], coef[32 + k] = 1j, 1
                for w in range(2):
                    out[kind, w, 0, :, sy, w, 0, k] = coef.real
                    out[kind, w, 1, :, sy, w, 0, k] = -coef.imag
                    out[kind, w, 0, :, sy, w, 1, k] = coef.imag
                    out[kind, w, 1, :, sy, w, 1, k] = coef.real
    return (out.reshape(3, 512, 256) * scale).astype(ml_dtypes.bfloat16)


def all_tables():
    wx, wy = plane_tables()
    wz, wz2, wzb, wzb2 = depth_tables()
    m01, m2, mx = time_tables()
    pieces = {
        "wx": wx, "wy": wy.reshape(160, 256), "m01": m01.reshape(1024, 256), "m2": np.concatenate([m2[0], m2[1]], 1),
        "lanes": lane_tables().reshape(1536, 256), "wzb": wzb, "wzb2": wzb2,
    }
    for name, table in (("wz", wz), ("wz2", wz2), ("mx", mx)):
        wide = np.concatenate([table, np.zeros((len(table), -table.shape[1] % 256), ml_dtypes.bfloat16)], 1)
        pieces[name] = np.concatenate([wide[:, :256], wide[:, 256:]], 0)
    first, at = {}, 0
    for name, table in pieces.items():
        first[name] = at
        at += len(table)
    return np.concatenate(list(pieces.values()), 0), first


def split(values):
    high = values.astype(BF)
    return high, (values - high.astype(F32)).astype(BF)


def dot(a, b):
    return jnp.dot(a, b, preferred_element_type=F32)


def owner(g, u):
    return jnp.where(u < 2, 2 * g + u, jnp.where(g == 0, 32, 64 - 2 * g) + u - 2)


def place(s):
    b, h = s // 2, s % 2
    g = jnp.where(b < 16, b, jnp.where(b == 16, 0, 32 - b))
    return g, jnp.where(b < 16, h, 2 + h)


def kernel(
    at_of, field, tables, out,
    planes, rows, rows_x, wx, wy, wz, wz2, wzb, wzb2, m01, m2, mx, lanes, lanes_b,
    send_a, send_b, recv_a, recv_b, time_send, time_send_x, time_sb, time_sbx,
    time_recv, time_recv_x, time_rb, time_rbx, sorts, last, blocks,
    field_sem, const_sem, ssa, rsa, ssx, rsx, ssb, rsb, sst, rst, sstx, rstx, sstb, rstb, sstbx, rstbx, ssl, rsl,
):
    s, tm = lax.axis_index("space"), lax.axis_index("tm")
    g, u = place(s)
    e = 4 * u + tm
    zero_g, zero_e, zero_u = g == 0, e == 0, u == 0
    pick_e, pick_g = jnp.where(zero_e, 1, 0), jnp.where(zero_g, 1, 0)

    def field_copy(pair):
        two = pl.ds(2 * pair, 2)
        return pltpu.make_async_copy(field.at[two], planes.at[two], field_sem.at[pair])

    def table_copy(i, dst, name, skip=0, columns=slice(None)):
        rows_at = pl.ds(pl.multiple_of(at_of[name] + skip, 16), dst.shape[0])
        return pltpu.make_async_copy(tables.at[rows_at, columns], dst, const_sem.at[i])

    consts = [
        table_copy(0, wx, "wx"),
        table_copy(1, wy, "wy"),
        table_copy(2, wz.at[:, :256], "wz"),
        table_copy(3, wz.at[:, 256:], "wz", 256),
        table_copy(4, wzb, "wzb"),
        table_copy(5, wzb2, "wzb2"),
        table_copy(6, m01, "m01", 512 * pick_e),
        table_copy(7, m2, "m2", 0, pl.ds(pl.multiple_of(128 * pick_e, 128), 128)),
        table_copy(8, mx.at[:, :256], "mx"),
        table_copy(9, mx.at[:, 256:], "mx", 768, slice(0, 128)),
        table_copy(10, lanes, "lanes", 512 * pick_g),
        table_copy(11, lanes_b, "lanes", 1024),
        table_copy(12, wz2.at[:, :256], "wz2"),
        table_copy(13, wz2.at[:, 256:], "wz2", 256),
    ]
    consts[0].start()
    field_copy(0).start()
    consts[1].start()

    barrier = pltpu.get_barrier_semaphore()

    def greet(space, time):
        pl.semaphore_signal(barrier, inc=1, device_id={"space": space, "tm": time}, device_id_type=MESH)


    def turn(value, count):
        return jnp.where(value >= count, value - count, value)

    place_x, place_y, place_z = s // 32, (s // 8) % 4, s % 8
    along = (
        [32 * turn(place_x + d, 2) for d in range(2)],
        [8 * turn(place_y + d, 4) for d in range(4)],
        [turn(place_z + d, 8) for d in range(8)],
    )
    others = [along[0][x] + along[1][y] + along[2][z] for x, y, z in OFFSETS]
    for to in others:
        greet(to, tm)

    for j in range(1, TM):
        greet(s, turn(tm + j, TM))
        for v in range(1, 4):
            greet(owner(g, turn(u + v, 4)), turn(tm + j, TM))

    for pair in range(1, CH // 2):
        field_copy(pair).start()
    for copy in consts[2:]:
        copy.start()

    rows_x[...] = jnp.zeros_like(rows_x)
    send_b[...] = jnp.zeros_like(send_b)

    def plane_step(ng, first, n):
        products = []
        for t in range(4):
            for pair in range(2):
                high, low = split(jnp.concatenate([planes[n, t, 2 * pair], planes[n, t, 2 * pair + 1]], axis=1))
                both = dot(wx[...], jnp.concatenate([high, low], axis=0))
                products.append((t, pair, both[:40] + both[40:]))
        for t, pair, both in products:
            at = pl.multiple_of(((n - first) * 4 + t) * 8, 8)
            for half in range(2):
                z = 2 * pair + half
                part = both[:, 128 * half : 128 * half + 128]
                for v in range(4):
                    tile = part[8 * v : 8 * v + 8]
                    if ng < 2:
                        rows[ng, z, pl.ds(v * 128 + at, 8), :] = tile
                    else:
                        rows[2, half, pl.ds(v * 128 + pair * 64 + at, 8), :] = tile
                rows_x[half, pl.ds(64 * pair + 4 * n + t, 1), :] = part[32:33]

    def along_y(values, side):
        high, low = split(values)
        both = lax.dot_general(
            wy[80 * side : 80 * side + 80, :], jnp.concatenate([high, low], axis=1), (((1,), (1,)), ((), ())),
            preferred_element_type=F32,
        )
        return both[:40] + both[40:]

    def exchange(ng):
        count = 4 if ng < 2 else 2
        products = [
            (z, side, along_y(rows[ng, z, 256 * side : 256 * side + 256, :], side)) for z in range(count) for side in range(2)
        ]
        extras = [along_y(rows_x[z], 0) for z in range(2)] if ng == 2 else []
        for z, side, both in products:
            for h in range(2):
                lanes_h = slice(128 * h, 128 * h + 128)
                for c in range(2):
                    at = (side * 32 + h) * STEP + 8 * ng + count * c + z
                    send_a[pl.ds(at, 16, stride=2 * STEP), :] = both[16 * c : 16 * c + 16, lanes_h]
                send_b[pl.ds((2 * side + h) * 12 + 4 * ng + z, 1), :] = both[32:33, lanes_h]
        for z, both in enumerate(extras):
            for c in range(2):
                send_a[pl.ds(20 + 2 * c + z, 16, stride=2 * STEP), :] = both[16 * c : 16 * c + 16]
            send_b[pl.ds(10 + z, 1), :] = both[32:33]

    def sent(move):
        first, end = MOVES[move]
        return 8 * first, 8 * (end - first) - (4 if end == 3 else 0)

    def sent_b(move):
        first, end = MOVES[move]
        return 4 * first, 4 * (end - first)

    def remote(src, dst, send_sem, recv_sem, space, time):
        return pltpu.make_async_remote_copy(
            src_ref=src, dst_ref=dst, send_sem=send_sem, recv_sem=recv_sem,
            device_id={"space": space, "tm": time}, device_id_type=MESH,
        )

    def space_copy(move, to):
        first, count = sent(move)
        src = pl.ds(pl.multiple_of(to * STEP + first, 8), count)
        return remote(send_a.at[src], recv_a.at[s, pl.ds(first, count)], ssa.at[move], rsa.at[move], to, tm)

    def send_space(move):
        first, count = sent(move)
        here = (s, pl.ds(first, count))
        last_move = move == len(MOVES) - 1

        for to in others:
            space_copy(move, to).start()

        if last_move:
            here_x = (s, pl.ds(20, 4))

            @pl.loop(0, 16)
            def _(k):
                @pl.when(2 * k != s)
                def _():
                    src = pl.ds(pl.multiple_of(2 * k * STEP + 20, 4), 4)
                    remote(send_a.at[src], recv_a.at[here_x], ssx.at[0], rsx.at[0], 2 * k, tm).start()

            @pl.when(zero_u)
            def _():
                recv_a[here_x] = send_a[pl.ds(pl.multiple_of(s * STEP + 20, 4), 4), :]

        first_b, count_b = sent_b(move)
        here_b = (s, pl.ds(first_b, count_b))
        for v, to in enumerate((0, 1, 32, 33)):
            src = pl.ds(12 * v + first_b, count_b)

            @pl.when(s != to)
            def _():
                remote(send_b.at[src], recv_b.at[here_b], ssb.at[move], rsb.at[move], to, tm).start()

            @pl.when(s == to)
            def _():
                recv_b[here_b] = send_b[src, :]

        recv_a[here] = send_a[pl.ds(pl.multiple_of(s * STEP + first, 8), count), :]

    consts[0].wait()
    for ng, (first, count) in enumerate(GROUPS):
        @pl.loop(first, first + count, step=2)
        def _(n):
            field_copy(n // 2).wait()
            plane_step(ng, first, n)
            plane_step(ng, first, n + 1)

        if ng == 0:
            consts[1].wait()
        exchange(ng)
        if ng == 0:
            pl.semaphore_wait(barrier, 63 + 3 + 9)
        for move, (_, end) in enumerate(MOVES):
            if ng == end - 1:
                send_space(move)

    for copy in consts[2:]:
        copy.wait()

    def wait_rows(rows_of, count, sem):
        pltpu.make_async_copy(rows_of.at[pl.ds(0, count)], rows_of.at[pl.ds(0, count)], sem).wait()

    def moved(move):
        first, end = MOVES[move]
        return TIME_AT[first], TIME_AT[end] - TIME_AT[first]

    def keep_time(ng, sort, z_rows, src, src_x):
        count = (TIME_AT[ng + 1] - TIME_AT[ng]) // 2
        sort[...] = z_rows
        for v in range(TM):
            for c in range(2):
                at = 80 * v + TIME_AT[ng] + count * c
                src[at : at + count, :] = sort[pl.ds(2 * v + c, count, stride=8), :]
        if ng == 2:
            src_x[...] = z_rows[64:104]

    def send_time(move, src, src_x, dst, dst_x, send_sem, recv_sem, send_sem_x, recv_sem_x):
        first, count = moved(move)
        mine = pl.ds(pl.multiple_of(tm * 80 + first, 8), count)
        here = (tm, pl.ds(first, count))
        for j in range(1, TM):
            to = tm + j
            to = jnp.where(to >= TM, to - TM, to)
            there = pl.ds(pl.multiple_of(to * 80 + first, 8), count)
            remote(src.at[there], dst.at[here], send_sem.at[move], recv_sem.at[move], s, to).start()
        dst[here] = src[mine, :]
        if move == len(MOVES) - 1:
            at_x = pl.ds(pl.multiple_of(tm * 40, 8), 40)

            @pl.when(jnp.logical_and(zero_u, tm != 0))
            def _():
                remote(src_x, dst_x.at[at_x], send_sem_x.at[0], recv_sem_x.at[0], s, 0).start()

            @pl.when(zero_e)
            def _():
                dst_x[pl.ds(0, 40), :] = src_x[...]

    time_a = (time_send, time_send_x, time_recv, time_recv_x, sst, rst, sstx, rstx)
    time_b = (time_sb, time_sbx, time_rb, time_rbx, sstb, rstb, sstbx, rstbx)

    def received(ref, ng):
        size = ref.shape[1] // 3
        count = SPACE * size
        values = ref[:, size * ng : size * ng + size, :].reshape(count, 128) if ng < 2 else None
        if ng == 2:
            count //= 2
            main, extra = (
                ref[:, at : at + size // 2, :].reshape(count, 128) for at in (2 * size, 2 * size + size // 2)
            )
            lower = lax.broadcasted_iota(jnp.int32, (count, 128), 1) < 64
            values = jnp.concatenate(
                [jnp.where(lower, main, pltpu.roll(extra, 64, 1)), jnp.where(lower, pltpu.roll(main, 64, 1), extra)], axis=0
            )
        high, low = split(values)
        return jnp.concatenate([high, low], axis=1)

    def depth_step(move):
        first, end = MOVES[move]
        wait_rows(send_a, 63 * sent(move)[1], rsa.at[move])
        if end == 3:
            @pl.when(zero_u)
            def _():
                wait_rows(send_a, 63 * 4, rsx.at[0])

        z_rows = []
        for ng in range(first, end):
            both = dot(wz[...] if ng < 2 else wz2[...], received(recv_a, ng))
            z_rows.append((both[:128, :128] + both[:128, 128:] + both[128:, :128]).T)
        for ng in range(first, end):
            keep_time(ng, sorts.at[ng], z_rows[ng - first], *time_a[:2])
        send_time(move, *time_a)

        @pl.when(zero_g)
        def _():
            wait_rows(send_a, 63 * sent_b(move)[1], rsb.at[move])
            z_rows = []
            for ng in range(first, end):
                both = dot(wzb[...] if ng < 2 else wzb2[...], received(recv_b, ng))
                both = both[:64, :128] + both[:64, 128:] + both[64:, :128]
                z_rows.append(jnp.concatenate([both, jnp.zeros_like(both)], axis=0).T)
            for ng in range(first, end):
                keep_time(ng, sorts.at[3 + ng], z_rows[ng - first], *time_b[:2])
            send_time(move, *time_b)

    def finish(values, table, signs):
        high, low = split(values)
        fill = table.shape[1] - 2 * values.shape[0]
        parts = [high, low] + ([jnp.zeros((fill, 128), BF)] if fill else [])
        both = dot(table[...], jnp.concatenate(parts, axis=0))
        both = both[: both.shape[0] // 2] + both[both.shape[0] // 2 :]
        count = both.shape[0] // 4
        pairs = [split(both[count * i : count * i + count]) for i in range(4)]
        both = jnp.concatenate([jnp.concatenate([pair[i] for pair in pairs], axis=1) for i in range(2)], axis=0)
        both = dot(both, signs[...])
        return both[:count] + both[count:]

    def keep(ng, value, first, add):
        for i in range(value.shape[0] // 8):
            for sy in range(2):
                j = 8 * sy + first + i
                part = value[8 * i : 8 * i + 8, 128 * sy : 128 * sy + 128]
                at = slice(j * STEP + 8 * ng, j * STEP + 8 * ng + 8)
                last[at, :] = last[at, :] + part if add else part

    def slot_of(sx):
        return jnp.where(sx == 0, e, jnp.where(zero_e, 0, 16 - e))

    def last_copy(j, first, count):
        at = pl.ds(pl.multiple_of(slot_of((j // 4) % 2) * STEP + first, 8), count)
        src = pl.ds(pl.multiple_of(j * STEP + first, 8), count)
        return remote(last.at[src], blocks.at[at], ssl.at[0], rsl.at[0], owner(g, j // 4), j % 4)

    def steps_of(ref, ng):
        count = TIME_AT[ng + 1] - TIME_AT[ng]
        return ref[:, TIME_AT[ng] : TIME_AT[ng + 1], :].reshape(TM * count, 128)

    def time_step(move):
        first, end = MOVES[move]
        rows_at, rows_count = 8 * first, 8 * (end - first)

        def finish_all(ref, ref_x, signs, recv_sem_x, add):
            values = [finish(steps_of(ref, ng), m01 if ng < 2 else m2, signs) for ng in range(first, end)]
            for ng in range(first, end):
                keep(ng, values[ng - first], 0, add)
            if end == 3:
                @pl.when(zero_e)
                def _():
                    wait_rows(time_recv_x, 120, recv_sem_x.at[0])
                    value = finish_x(ref_x, signs)
                    for i in range(3):
                        keep(i, value[32 * i : 32 * i + 32], 4, True)

        wait_rows(time_send, 3 * moved(move)[1], rst.at[move])
        finish_all(time_recv, time_recv_x, lanes, rstx, False)

        @pl.when(zero_g)
        def _():
            wait_rows(time_sb, 3 * moved(move)[1], rstb.at[move])
            finish_all(time_rb, time_rbx, lanes_b, rstbx, True)

        @pl.when(jnp.logical_not(zero_e))
        def _():
            side = jnp.where(e >= 8, 8, 0)
            for k in range(8):
                last_copy(8 - side + k, rows_at, rows_count).start()
            for k in range(1, 8):
                last_copy(side + turn(e - side + k, 8), rows_at, rows_count).start()

        @pl.when(zero_e)
        def _():
            for j in (8, 9, 10, 11, 1, 2, 3):
                last_copy(j, rows_at, rows_count).start()
            if end == 3:
                for j in (12, 13, 14, 15, 4, 5, 6, 7):
                    last_copy(j, 0, STEP).start()

        at = pl.ds(pl.multiple_of(slot_of(u % 2) * STEP + rows_at, 8), rows_count)
        blocks[at, :] = last[pl.ds(pl.multiple_of(e * STEP + rows_at, 8), rows_count), :]

    def finish_x(ref, signs):
        high, low = split(ref[...])
        both = dot(mx[...], jnp.concatenate([high, low, jnp.zeros((64, 128), BF)], axis=0))
        both = both[:384] + both[384:]
        values = []
        for i in range(3):
            pairs = [split(both[128 * i + 32 * j : 128 * i + 32 * j + 32]) for j in range(4)]
            value = jnp.concatenate([jnp.concatenate([pair[h] for pair in pairs], axis=1) for h in range(2)], axis=0)
            value = dot(value, signs[...])
            values.append(value[:32] + value[32:])
        return jnp.concatenate(values, axis=0)

    for move in range(len(MOVES)):
        depth_step(move)
        time_step(move)

    wait_rows(blocks, 15 * STEP, rsl.at[0])
    for ng in range(3):
        for r in range(8):
            q, rest = r // 2, r % 2
            if ng == 2 and rest:
                continue
            value = blocks[pl.ds(8 * ng + r, 16, stride=STEP), :]
            for half in range(2):
                n = 4 * ng + 2 * half + rest if ng < 2 else 8 + half
                for part in range(2):
                    at = 64 * half + 32 * part
                    out[part, n, q] = value[:, at : at + 32]

    wait_rows(blocks, 15 * STEP, ssl.at[0])
    for move, (first, end) in enumerate(MOVES):
        wait_rows(send_a, 63 * sent(move)[1], ssa.at[move])

        @pl.when(zero_g)
        def _():
            wait_rows(send_b, 3 * sent_b(move)[1], ssb.at[move])

        @pl.when(jnp.logical_not(zero_g))
        def _():
            wait_rows(send_b, 4 * sent_b(move)[1], ssb.at[move])

    for move in range(len(MOVES)):
        wait_rows(time_send, 3 * moved(move)[1], sst.at[move])

        @pl.when(zero_g)
        def _():
            wait_rows(time_sb, 3 * moved(move)[1], sstb.at[move])

    @pl.when(zero_u)
    def _():
        wait_rows(send_a, 15 * 4, ssx.at[0])

    @pl.when(jnp.logical_not(zero_u))
    def _():
        wait_rows(send_a, 16 * 4, ssx.at[0])

    @pl.when(jnp.logical_and(zero_u, tm != 0))
    def _():
        wait_rows(time_send_x, 40, sstx.at[0])

        @pl.when(zero_g)
        def _():
            wait_rows(time_sbx, 40, sstbx.at[0])


def body(field):
    tables, at_of = all_tables()
    dma = pltpu.SemaphoreType.DMA

    def vmem(*shape):
        return pltpu.VMEM(shape, F32)

    def table(*shape):
        return pltpu.VMEM(shape, BF)

    return pl.pallas_call(
        functools.partial(kernel, at_of),
        out_shape=jax.ShapeDtypeStruct((2, CH, 4, 16, 32), F32),
        in_specs=[pl.BlockSpec(memory_space=pltpu.HBM)] * 2,
        out_specs=pl.BlockSpec(memory_space=pltpu.VMEM),
        scratch_shapes=[
            vmem(CH, 4, 4, 128, 128),
            vmem(3, 4, 512, 128), vmem(2, 128, 128),
            table(80, 256), table(160, 256), table(256, 512), table(256, 512), table(128, 256), table(128, 256),
            table(512, 256), table(512, 128), table(768, 384),
            table(512, 256), table(512, 256),
            vmem(64 * STEP, 128), vmem(48, 128), vmem(64, STEP, 128), vmem(64, 12, 128),
            vmem(320, 128), vmem(40, 128), vmem(320, 128), vmem(40, 128),
            vmem(4, 80, 128), vmem(160, 128), vmem(4, 80, 128), vmem(160, 128),
            vmem(6, 128, 128), vmem(16 * STEP, 128), vmem(16 * STEP, 128),
            dma((CH // 2,)), dma((14,)),
            dma((len(MOVES),)), dma((len(MOVES),)), dma((1,)), dma((1,)), dma((len(MOVES),)), dma((len(MOVES),)),
            dma((len(MOVES),)), dma((len(MOVES),)), dma((1,)), dma((1,)),
            dma((len(MOVES),)), dma((len(MOVES),)), dma((1,)), dma((1,)),
            dma((1,)), dma((1,)),
        ],
        compiler_params=pltpu.CompilerParams(
            collective_id=0, has_side_effects=True, vmem_limit_bytes=52 * 1024 * 1024
        ),
        cost_estimate=pl.CostEstimate(flops=20_000_000_000, bytes_accessed=13_000_000, transcendentals=0),
    )(field, tables)


def solution(mesh):
    return jax.shard_map(
        body,
        mesh=mesh,
        in_specs=(P(None, "tm", "space", None, None),),
        out_specs=P(None, None, "tm", "space", None),
        check_vma=False,
    )
```

```python
import functools
import math

import jax
import jax.numpy as jnp
import ml_dtypes
import numpy as np
from jax import lax
from jax.experimental import pallas as pl
from jax.experimental.pallas import tpu as pltpu
from jax.sharding import PartitionSpec as P

MESH = pl.DeviceIdType.MESH
BF = jnp.bfloat16
F32 = jnp.float32

CH = 10
NX = 128
NY = 128
NT = 16
NZ = 256
SPACE = 64
TM = 4
GROUPS = ((0, 4), (4, 4), (8, 2))
STEP = 24
MOVES = ((0, 1), (1, 3))
OFFSETS = sorted(
    [(k // 32, (k // 8) % 4, k % 8) for k in range(1, SPACE)],
    key=lambda at: (-2 * at[0] - min(at[1], 4 - at[1]) - min(at[2], 8 - at[2]), at[1], at[2]),
)
TIME_AT = (0, 32, 64, 80)


def halves(table):
    high = table.astype(ml_dtypes.bfloat16)
    low = (table - high.astype(np.float64)).astype(ml_dtypes.bfloat16)
    return high, low


def angle(freq, pos, length):
    return 2.0 * math.pi * ((freq * pos) % length) / length


def real_modes(order):
    cells = np.arange(128)
    rows = np.zeros((40, 128))
    for e in range(16):
        rows[order(e, 0)] = np.cos(angle(e, cells, 128))
        rows[order(e, 1)] = np.sin(angle(e, cells, 128)) if e else np.cos(angle(16, cells, 128))
    rows[32] = np.sin(angle(16, cells, 128))
    return rows


def plane_tables():
    def build(order):
        high, low = halves(real_modes(order))
        return np.concatenate([np.concatenate([high, high], 1), np.concatenate([low, low], 1)], 0)

    wx = build(lambda e, c: 2 * e + c)
    up = build(lambda e, c: 16 * c + e)
    down = build(lambda e, c: 16 * c + (16 - e) % 16)
    return wx, np.stack([up, down])


def depth_tables():
    depth = np.arange(NZ)
    k = np.arange(32)[:, None]
    both = np.concatenate([np.cos(angle(k, depth, NZ)), np.sin(angle(k, depth, NZ))], 0)
    main = np.zeros((2, 64, SPACE, 2, 4))
    for c in range(2):
        main[c, :, :, c, :] = both.reshape(64, SPACE, 4)
    main = main.reshape(128, 512)
    main2 = main.reshape(-1, SPACE, 2, 2, 2).transpose(0, 3, 1, 2, 4).reshape(-1, 512)
    both2 = both.reshape(-1, SPACE, 2, 2).transpose(0, 2, 1, 3).reshape(-1, 256)
    return [np.concatenate(halves(table), 0) for table in (main, main2, both, both2)]


def time_tables():
    def phase(q, step):
        return np.exp(-1j * angle(q if q < 8 else q - 16, step, NT))

    def pack(table, pad):
        high, low = halves(table)
        blank = np.zeros(table.shape[:-1] + (pad,), ml_dtypes.bfloat16)
        return np.concatenate([np.concatenate([part, part, blank], -1) for part in (high, low)], -2)

    out = []
    for count in (4, 2):
        table = np.zeros((2, 2, 2, 2, TM, 8, TM, 2, count, 4))
        for n in range(count):
            half, rest = divmod(n, count // 2)
            for q in range(16):
                for step in range(16):
                    value = phase(q, step)
                    for sx, sign in ((0, 1), (1, -1)):
                        at = (sx, q // 4, (q % 4) * 2 + rest, step // 4)
                        for zero in range(2):
                            if zero:
                                terms = ((sx, value),)
                            else:
                                terms = ((0, value), (1, -1j * sign * value))
                            for c, term in terms:
                                table[(zero, half, 0) + at + (c, n, step % 4)] = term.real
                                table[(zero, half, 1) + at + (c, n, step % 4)] = term.imag
        out.append(pack(table.reshape(2, 256, 32 * count), 0))
    table = np.zeros((3, 2, 2, TM, 8, TM, CH, 4))
    for n in range(CH):
        ng = n // 4
        half, rest = divmod(n % 4, 2) if ng < 2 else (n - 8, 0)
        for q in range(16):
            for step in range(16):
                term = 1j * phase(q, step)
                at = (q // 4, (q % 4) * 2 + rest, step // 4, n, step % 4)
                table[(ng, half, 0) + at] = term.real
                table[(ng, half, 1) + at] = term.imag
    out.append(pack(table.reshape(384, 160), 64))
    return out


def lane_tables():
    scale = 1.0 / math.sqrt(NX * NY * NZ * NT)
    out = np.zeros((3, 2, 2, 128, 2, 2, 2, 32))
    for sy, sign in ((0, 1), (1, -1)):
        for k in range(32):
            for kind in range(3):
                coef = np.zeros(128, complex)
                if kind == 0:
                    coef[k], coef[32 + k] = 1, -1j
                    coef[64 + k], coef[96 + k] = -1j * sign, -sign
                elif kind == 1:
                    at = 64 * sy
                    coef[at + k], coef[at + 32 + k] = 1, -1j
                elif sy == 1:
                    coef[k], coef[32 + k] = 1j, 1
                for w in range(2):
                    out[kind, w, 0, :, sy, w, 0, k] = coef.real
                    out[kind, w, 1, :, sy, w, 0, k] = -coef.imag
                    out[kind, w, 0, :, sy, w, 1, k] = coef.imag
                    out[kind, w, 1, :, sy, w, 1, k] = coef.real
    return (out.reshape(3, 512, 256) * scale).astype(ml_dtypes.bfloat16)


def all_tables():
    wx, wy = plane_tables()
    wz, wz2, wzb, wzb2 = depth_tables()
    m01, m2, mx = time_tables()
    pieces = {
        "wx": wx, "wy": wy.reshape(160, 256), "m01": m01.reshape(1024, 256), "m2": np.concatenate([m2[0], m2[1]], 1),
        "lanes": lane_tables().reshape(1536, 256), "wzb": wzb, "wzb2": wzb2,
    }
    for name, table in (("wz", wz), ("wz2", wz2), ("mx", mx)):
        wide = np.concatenate([table, np.zeros((len(table), -table.shape[1] % 256), ml_dtypes.bfloat16)], 1)
        pieces[name] = np.concatenate([wide[:, :256], wide[:, 256:]], 0)
    first, at = {}, 0
    for name, table in pieces.items():
        first[name] = at
        at += len(table)
    return np.concatenate(list(pieces.values()), 0), first


def split(values):
    high = values.astype(BF)
    return high, (values - high.astype(F32)).astype(BF)


def split_wide(values):
    scaled = values * 65537.0
    high = scaled - (scaled - values)
    return high, values - high


def dot(a, b):
    return jnp.dot(a, b, preferred_element_type=F32)


def owner(g, u):
    return jnp.where(u < 2, 2 * g + u, jnp.where(g == 0, 32, 64 - 2 * g) + u - 2)


def place(s):
    b, h = s // 2, s % 2
    g = jnp.where(b < 16, b, jnp.where(b == 16, 0, 32 - b))
    return g, jnp.where(b < 16, h, 2 + h)


def kernel(
    at_of, field, tables, out,
    planes, rows, rows_x, wx, wy, wz, wz2, wzb, wzb2, m01, m2, mx, lanes, lanes_b,
    send_a, send_b, recv_a, recv_b, time_send, time_send_x, time_sb, time_sbx,
    time_recv, time_recv_x, time_rb, time_rbx, sorts, last, blocks,
    field_sem, const_sem, ssa, rsa, ssx, rsx, ssb, rsb, sst, rst, sstx, rstx, sstb, rstb, sstbx, rstbx, ssl, rsl,
):
    s, tm = lax.axis_index("space"), lax.axis_index("tm")
    g, u = place(s)
    e = 4 * u + tm
    zero_g, zero_e, zero_u = g == 0, e == 0, u == 0
    pick_e, pick_g = jnp.where(zero_e, 1, 0), jnp.where(zero_g, 1, 0)

    def field_copy(pair):
        two = pl.ds(2 * pair, 2)
        return pltpu.make_async_copy(field.at[two], planes.at[two], field_sem.at[pair])

    def table_copy(i, dst, name, skip=0, columns=slice(None)):
        rows_at = pl.ds(pl.multiple_of(at_of[name] + skip, 16), dst.shape[0])
        return pltpu.make_async_copy(tables.at[rows_at, columns], dst, const_sem.at[i])

    consts = [
        table_copy(0, wx, "wx"),
        table_copy(1, wy, "wy"),
        table_copy(2, wz.at[:, :256], "wz"),
        table_copy(3, wz.at[:, 256:], "wz", 256),
        table_copy(4, wzb, "wzb"),
        table_copy(5, wzb2, "wzb2"),
        table_copy(6, m01, "m01", 512 * pick_e),
        table_copy(7, m2, "m2", 0, pl.ds(pl.multiple_of(128 * pick_e, 128), 128)),
        table_copy(8, mx.at[:, :256], "mx"),
        table_copy(9, mx.at[:, 256:], "mx", 768, slice(0, 128)),
        table_copy(10, lanes, "lanes", 512 * pick_g),
        table_copy(11, lanes_b, "lanes", 1024),
        table_copy(12, wz2.at[:, :256], "wz2"),
        table_copy(13, wz2.at[:, 256:], "wz2", 256),
    ]
    consts[0].start()
    field_copy(0).start()
    consts[1].start()

    barrier = pltpu.get_barrier_semaphore()

    def greet(space, time):
        pl.semaphore_signal(barrier, inc=1, device_id={"space": space, "tm": time}, device_id_type=MESH)


    def turn(value, count):
        return jnp.where(value >= count, value - count, value)

    place_x, place_y, place_z = s // 32, (s // 8) % 4, s % 8
    along = (
        [32 * turn(place_x + d, 2) for d in range(2)],
        [8 * turn(place_y + d, 4) for d in range(4)],
        [turn(place_z + d, 8) for d in range(8)],
    )
    others = [along[0][x] + along[1][y] + along[2][z] for x, y, z in OFFSETS]
    for to in others:
        greet(to, tm)

    for j in range(1, TM):
        greet(s, turn(tm + j, TM))
        for v in range(1, 4):
            greet(owner(g, turn(u + v, 4)), turn(tm + j, TM))

    for pair in range(1, CH // 2):
        field_copy(pair).start()
    for copy in consts[2:]:
        copy.start()

    rows_x[...] = jnp.zeros_like(rows_x)
    send_b[...] = jnp.zeros_like(send_b)

    def plane_step(ng, first, n):
        wx_wide = wx[...].astype(F32)
        products = []
        for t in range(4):
            for pair in range(2):
                high, low = split_wide(jnp.concatenate([planes[n, t, 2 * pair], planes[n, t, 2 * pair + 1]], axis=1))
                both = dot(wx_wide, jnp.concatenate([high, low], axis=0))
                products.append((t, pair, both[:40] + both[40:]))
        for t, pair, both in products:
            at = pl.multiple_of(((n - first) * 4 + t) * 8, 8)
            for half in range(2):
                z = 2 * pair + half
                part = both[:, 128 * half : 128 * half + 128]
                for v in range(4):
                    tile = part[8 * v : 8 * v + 8]
                    if ng < 2:
                        rows[ng, z, pl.ds(v * 128 + at, 8), :] = tile
                    else:
                        rows[2, half, pl.ds(v * 128 + pair * 64 + at, 8), :] = tile
                rows_x[half, pl.ds(64 * pair + 4 * n + t, 1), :] = part[32:33]

    def along_y(values, side):
        high, low = split(values)
        both = lax.dot_general(
            wy[80 * side : 80 * side + 80, :], jnp.concatenate([high, low], axis=1), (((1,), (1,)), ((), ())),
            preferred_element_type=F32,
        )
        return both[:40] + both[40:]

    def exchange(ng):
        count = 4 if ng < 2 else 2
        products = [
            (z, side, along_y(rows[ng, z, 256 * side : 256 * side + 256, :], side)) for z in range(count) for side in range(2)
        ]
        extras = [along_y(rows_x[z], 0) for z in range(2)] if ng == 2 else []
        for z, side, both in products:
            for h in range(2):
                lanes_h = slice(128 * h, 128 * h + 128)
                for c in range(2):
                    at = (side * 32 + h) * STEP + 8 * ng + count * c + z
                    send_a[pl.ds(at, 16, stride=2 * STEP), :] = both[16 * c : 16 * c + 16, lanes_h]
                send_b[pl.ds((2 * side + h) * 12 + 4 * ng + z, 1), :] = both[32:33, lanes_h]
        for z, both in enumerate(extras):
            for c in range(2):
                send_a[pl.ds(20 + 2 * c + z, 16, stride=2 * STEP), :] = both[16 * c : 16 * c + 16]
            send_b[pl.ds(10 + z, 1), :] = both[32:33]

    def sent(move):
        first, end = MOVES[move]
        return 8 * first, 8 * (end - first) - (4 if end == 3 else 0)

    def sent_b(move):
        first, end = MOVES[move]
        return 4 * first, 4 * (end - first)

    def remote(src, dst, send_sem, recv_sem, space, time):
        return pltpu.make_async_remote_copy(
            src_ref=src, dst_ref=dst, send_sem=send_sem, recv_sem=recv_sem,
            device_id={"space": space, "tm": time}, device_id_type=MESH,
        )

    def space_copy(move, to):
        first, count = sent(move)
        src = pl.ds(pl.multiple_of(to * STEP + first, 8), count)
        return remote(send_a.at[src], recv_a.at[s, pl.ds(first, count)], ssa.at[move], rsa.at[move], to, tm)

    def send_space(move):
        first, count = sent(move)
        here = (s, pl.ds(first, count))
        last_move = move == len(MOVES) - 1

        for to in others:
            space_copy(move, to).start()

        if last_move:
            here_x = (s, pl.ds(20, 4))

            @pl.loop(0, 16)
            def _(k):
                @pl.when(2 * k != s)
                def _():
                    src = pl.ds(pl.multiple_of(2 * k * STEP + 20, 4), 4)
                    remote(send_a.at[src], recv_a.at[here_x], ssx.at[0], rsx.at[0], 2 * k, tm).start()

            @pl.when(zero_u)
            def _():
                recv_a[here_x] = send_a[pl.ds(pl.multiple_of(s * STEP + 20, 4), 4), :]

        first_b, count_b = sent_b(move)
        here_b = (s, pl.ds(first_b, count_b))
        for v, to in enumerate((0, 1, 32, 33)):
            src = pl.ds(12 * v + first_b, count_b)

            @pl.when(s != to)
            def _():
                remote(send_b.at[src], recv_b.at[here_b], ssb.at[move], rsb.at[move], to, tm).start()

            @pl.when(s == to)
            def _():
                recv_b[here_b] = send_b[src, :]

        recv_a[here] = send_a[pl.ds(pl.multiple_of(s * STEP + first, 8), count), :]

    consts[0].wait()
    for ng, (first, count) in enumerate(GROUPS):
        @pl.loop(first, first + count, step=2)
        def _(n):
            field_copy(n // 2).wait()
            plane_step(ng, first, n)
            plane_step(ng, first, n + 1)

        if ng == 0:
            consts[1].wait()
        exchange(ng)
        if ng == 0:
            pl.semaphore_wait(barrier, 63 + 3 + 9)
        for move, (_, end) in enumerate(MOVES):
            if ng == end - 1:
                send_space(move)

    for copy in consts[2:]:
        copy.wait()

    def wait_rows(rows_of, count, sem):
        pltpu.make_async_copy(rows_of.at[pl.ds(0, count)], rows_of.at[pl.ds(0, count)], sem).wait()

    def moved(move):
        first, end = MOVES[move]
        return TIME_AT[first], TIME_AT[end] - TIME_AT[first]

    def keep_time(ng, sort, z_rows, src, src_x):
        count = (TIME_AT[ng + 1] - TIME_AT[ng]) // 2
        sort[...] = z_rows
        for v in range(TM):
            for c in range(2):
                at = 80 * v + TIME_AT[ng] + count * c
                src[at : at + count, :] = sort[pl.ds(2 * v + c, count, stride=8), :]
        if ng == 2:
            src_x[...] = z_rows[64:104]

    def send_time(move, src, src_x, dst, dst_x, send_sem, recv_sem, send_sem_x, recv_sem_x):
        first, count = moved(move)
        mine = pl.ds(pl.multiple_of(tm * 80 + first, 8), count)
        here = (tm, pl.ds(first, count))
        for j in range(1, TM):
            to = tm + j
            to = jnp.where(to >= TM, to - TM, to)
            there = pl.ds(pl.multiple_of(to * 80 + first, 8), count)
            remote(src.at[there], dst.at[here], send_sem.at[move], recv_sem.at[move], s, to).start()
        dst[here] = src[mine, :]
        if move == len(MOVES) - 1:
            at_x = pl.ds(pl.multiple_of(tm * 40, 8), 40)

            @pl.when(jnp.logical_and(zero_u, tm != 0))
            def _():
                remote(src_x, dst_x.at[at_x], send_sem_x.at[0], recv_sem_x.at[0], s, 0).start()

            @pl.when(zero_e)
            def _():
                dst_x[pl.ds(0, 40), :] = src_x[...]

    time_a = (time_send, time_send_x, time_recv, time_recv_x, sst, rst, sstx, rstx)
    time_b = (time_sb, time_sbx, time_rb, time_rbx, sstb, rstb, sstbx, rstbx)

    def received(ref, ng):
        size = ref.shape[1] // 3
        count = SPACE * size
        values = ref[:, size * ng : size * ng + size, :].reshape(count, 128) if ng < 2 else None
        if ng == 2:
            count //= 2
            main, extra = (
                ref[:, at : at + size // 2, :].reshape(count, 128) for at in (2 * size, 2 * size + size // 2)
            )
            lower = lax.broadcasted_iota(jnp.int32, (count, 128), 1) < 64
            values = jnp.concatenate(
                [jnp.where(lower, main, pltpu.roll(extra, 64, 1)), jnp.where(lower, pltpu.roll(main, 64, 1), extra)], axis=0
            )
        high, low = split(values)
        return jnp.concatenate([high, low], axis=1)

    def depth_step(move):
        first, end = MOVES[move]
        wait_rows(send_a, 63 * sent(move)[1], rsa.at[move])
        if end == 3:
            @pl.when(zero_u)
            def _():
                wait_rows(send_a, 63 * 4, rsx.at[0])

        z_rows = []
        for ng in range(first, end):
            both = dot(wz[...] if ng < 2 else wz2[...], received(recv_a, ng))
            z_rows.append((both[:128, :128] + both[:128, 128:] + both[128:, :128]).T)
        for ng in range(first, end):
            keep_time(ng, sorts.at[ng], z_rows[ng - first], *time_a[:2])
        send_time(move, *time_a)

        @pl.when(zero_g)
        def _():
            wait_rows(send_a, 63 * sent_b(move)[1], rsb.at[move])
            z_rows = []
            for ng in range(first, end):
                both = dot(wzb[...] if ng < 2 else wzb2[...], received(recv_b, ng))
                both = both[:64, :128] + both[:64, 128:] + both[64:, :128]
                z_rows.append(jnp.concatenate([both, jnp.zeros_like(both)], axis=0).T)
            for ng in range(first, end):
                keep_time(ng, sorts.at[3 + ng], z_rows[ng - first], *time_b[:2])
            send_time(move, *time_b)

    def finish(values, table, signs):
        high, low = split(values)
        fill = table.shape[1] - 2 * values.shape[0]
        parts = [high, low] + ([jnp.zeros((fill, 128), BF)] if fill else [])
        both = dot(table[...], jnp.concatenate(parts, axis=0))
        both = both[: both.shape[0] // 2] + both[both.shape[0] // 2 :]
        count = both.shape[0] // 4
        pairs = [split(both[count * i : count * i + count]) for i in range(4)]
        both = jnp.concatenate([jnp.concatenate([pair[i] for pair in pairs], axis=1) for i in range(2)], axis=0)
        both = dot(both, signs[...])
        return both[:count] + both[count:]

    def keep(ng, value, first, add):
        for i in range(value.shape[0] // 8):
            for sy in range(2):
                j = 8 * sy + first + i
                part = value[8 * i : 8 * i + 8, 128 * sy : 128 * sy + 128]
                at = slice(j * STEP + 8 * ng, j * STEP + 8 * ng + 8)
                last[at, :] = last[at, :] + part if add else part

    def slot_of(sx):
        return jnp.where(sx == 0, e, jnp.where(zero_e, 0, 16 - e))

    def last_copy(j, first, count):
        at = pl.ds(pl.multiple_of(slot_of((j // 4) % 2) * STEP + first, 8), count)
        src = pl.ds(pl.multiple_of(j * STEP + first, 8), count)
        return remote(last.at[src], blocks.at[at], ssl.at[0], rsl.at[0], owner(g, j // 4), j % 4)

    def steps_of(ref, ng):
        count = TIME_AT[ng + 1] - TIME_AT[ng]
        return ref[:, TIME_AT[ng] : TIME_AT[ng + 1], :].reshape(TM * count, 128)

    def time_step(move):
        first, end = MOVES[move]
        rows_at, rows_count = 8 * first, 8 * (end - first)

        def finish_all(ref, ref_x, signs, recv_sem_x, add):
            values = [finish(steps_of(ref, ng), m01 if ng < 2 else m2, signs) for ng in range(first, end)]
            for ng in range(first, end):
                keep(ng, values[ng - first], 0, add)
            if end == 3:
                @pl.when(zero_e)
                def _():
                    wait_rows(time_recv_x, 120, recv_sem_x.at[0])
                    value = finish_x(ref_x, signs)
                    for i in range(3):
                        keep(i, value[32 * i : 32 * i + 32], 4, True)

        wait_rows(time_send, 3 * moved(move)[1], rst.at[move])
        finish_all(time_recv, time_recv_x, lanes, rstx, False)

        @pl.when(zero_g)
        def _():
            wait_rows(time_sb, 3 * moved(move)[1], rstb.at[move])
            finish_all(time_rb, time_rbx, lanes_b, rstbx, True)

        @pl.when(jnp.logical_not(zero_e))
        def _():
            side = jnp.where(e >= 8, 8, 0)
            for k in range(8):
                last_copy(8 - side + k, rows_at, rows_count).start()
            for k in range(1, 8):
                last_copy(side + turn(e - side + k, 8), rows_at, rows_count).start()

        @pl.when(zero_e)
        def _():
            for j in (8, 9, 10, 11, 1, 2, 3):
                last_copy(j, rows_at, rows_count).start()
            if end == 3:
                for j in (12, 13, 14, 15, 4, 5, 6, 7):
                    last_copy(j, 0, STEP).start()

        at = pl.ds(pl.multiple_of(slot_of(u % 2) * STEP + rows_at, 8), rows_count)
        blocks[at, :] = last[pl.ds(pl.multiple_of(e * STEP + rows_at, 8), rows_count), :]

    def finish_x(ref, signs):
        high, low = split(ref[...])
        both = dot(mx[...], jnp.concatenate([high, low, jnp.zeros((64, 128), BF)], axis=0))
        both = both[:384] + both[384:]
        values = []
        for i in range(3):
            pairs = [split(both[128 * i + 32 * j : 128 * i + 32 * j + 32]) for j in range(4)]
            value = jnp.concatenate([jnp.concatenate([pair[h] for pair in pairs], axis=1) for h in range(2)], axis=0)
            value = dot(value, signs[...])
            values.append(value[:32] + value[32:])
        return jnp.concatenate(values, axis=0)

    for move in range(len(MOVES)):
        depth_step(move)
        time_step(move)

    wait_rows(blocks, 15 * STEP, rsl.at[0])
    for ng in range(3):
        for r in range(8):
            q, rest = r // 2, r % 2
            if ng == 2 and rest:
                continue
            value = blocks[pl.ds(8 * ng + r, 16, stride=STEP), :]
            for half in range(2):
                n = 4 * ng + 2 * half + rest if ng < 2 else 8 + half
                for part in range(2):
                    at = 64 * half + 32 * part
                    out[part, n, q] = value[:, at : at + 32]

    wait_rows(blocks, 15 * STEP, ssl.at[0])
    for move, (first, end) in enumerate(MOVES):
        wait_rows(send_a, 63 * sent(move)[1], ssa.at[move])

        @pl.when(zero_g)
        def _():
            wait_rows(send_b, 3 * sent_b(move)[1], ssb.at[move])

        @pl.when(jnp.logical_not(zero_g))
        def _():
            wait_rows(send_b, 4 * sent_b(move)[1], ssb.at[move])

    for move in range(len(MOVES)):
        wait_rows(time_send, 3 * moved(move)[1], sst.at[move])

        @pl.when(zero_g)
        def _():
            wait_rows(time_sb, 3 * moved(move)[1], sstb.at[move])

    @pl.when(zero_u)
    def _():
        wait_rows(send_a, 15 * 4, ssx.at[0])

    @pl.when(jnp.logical_not(zero_u))
    def _():
        wait_rows(send_a, 16 * 4, ssx.at[0])

    @pl.when(jnp.logical_and(zero_u, tm != 0))
    def _():
        wait_rows(time_send_x, 40, sstx.at[0])

        @pl.when(zero_g)
        def _():
            wait_rows(time_sbx, 40, sstbx.at[0])


def body(field):
    tables, at_of = all_tables()
    dma = pltpu.SemaphoreType.DMA

    def vmem(*shape):
        return pltpu.VMEM(shape, F32)

    def table(*shape):
        return pltpu.VMEM(shape, BF)

    return pl.pallas_call(
        functools.partial(kernel, at_of),
        out_shape=jax.ShapeDtypeStruct((2, CH, 4, 16, 32), F32),
        in_specs=[pl.BlockSpec(memory_space=pltpu.HBM)] * 2,
        out_specs=pl.BlockSpec(memory_space=pltpu.VMEM),
        scratch_shapes=[
            vmem(CH, 4, 4, 128, 128),
            vmem(3, 4, 512, 128), vmem(2, 128, 128),
            table(80, 256), table(160, 256), table(256, 512), table(256, 512), table(128, 256), table(128, 256),
            table(512, 256), table(512, 128), table(768, 384),
            table(512, 256), table(512, 256),
            vmem(64 * STEP, 128), vmem(48, 128), vmem(64, STEP, 128), vmem(64, 12, 128),
            vmem(320, 128), vmem(40, 128), vmem(320, 128), vmem(40, 128),
            vmem(4, 80, 128), vmem(160, 128), vmem(4, 80, 128), vmem(160, 128),
            vmem(6, 128, 128), vmem(16 * STEP, 128), vmem(16 * STEP, 128),
            dma((CH // 2,)), dma((14,)),
            dma((len(MOVES),)), dma((len(MOVES),)), dma((1,)), dma((1,)), dma((len(MOVES),)), dma((len(MOVES),)),
            dma((len(MOVES),)), dma((len(MOVES),)), dma((1,)), dma((1,)),
            dma((len(MOVES),)), dma((len(MOVES),)), dma((1,)), dma((1,)),
            dma((1,)), dma((1,)),
        ],
        compiler_params=pltpu.CompilerParams(
            collective_id=0, has_side_effects=True, vmem_limit_bytes=52 * 1024 * 1024
        ),
        cost_estimate=pl.CostEstimate(flops=20_000_000_000, bytes_accessed=13_000_000, transcendentals=0),
    )(field, tables)


def solution(mesh):
    return jax.shard_map(
        body,
        mesh=mesh,
        in_specs=(P(None, "tm", "space", None, None),),
        out_specs=P(None, None, "tm", "space", None),
        check_vma=False,
    )
```

```python
import functools
import math

import jax
import jax.numpy as jnp
import ml_dtypes
import numpy as np
from jax import lax
from jax.experimental import pallas as pl
from jax.experimental.pallas import tpu as pltpu
from jax.sharding import PartitionSpec as P

MESH = pl.DeviceIdType.MESH
BF = jnp.bfloat16
F32 = jnp.float32

CH = 10
NX = 128
NY = 128
NT = 16
NZ = 256
SPACE = 64
TM = 4
GROUPS = ((0, 4), (4, 4), (8, 2))
STEP = 24
MOVES = ((0, 1), (1, 3))
OFFSETS = sorted(
    [(k // 32, (k // 8) % 4, k % 8) for k in range(1, SPACE)],
    key=lambda at: (-min(at[1], 4 - at[1]) - min(at[2], 8 - at[2]), at[1], at[2], at[0]),
)
TIME_AT = (0, 32, 64, 80)


def halves(table):
    high = table.astype(ml_dtypes.bfloat16)
    low = (table - high.astype(np.float64)).astype(ml_dtypes.bfloat16)
    return high, low


def angle(freq, pos, length):
    return 2.0 * math.pi * ((freq * pos) % length) / length


def real_modes(order):
    cells = np.arange(128)
    rows = np.zeros((40, 128))
    for e in range(16):
        rows[order(e, 0)] = np.cos(angle(e, cells, 128))
        rows[order(e, 1)] = np.sin(angle(e, cells, 128)) if e else np.cos(angle(16, cells, 128))
    rows[32] = np.sin(angle(16, cells, 128))
    return rows


def plane_tables():
    def build(order):
        high, low = halves(real_modes(order))
        return np.concatenate([np.concatenate([high, high], 1), np.concatenate([low, low], 1)], 0)

    wx = build(lambda e, c: 2 * e + c)
    up = build(lambda e, c: 16 * c + e)
    down = build(lambda e, c: 16 * c + (16 - e) % 16)
    return wx, np.stack([up, down])


def depth_tables():
    depth = np.arange(NZ)
    k = np.arange(32)[:, None]
    both = np.concatenate([np.cos(angle(k, depth, NZ)), np.sin(angle(k, depth, NZ))], 0)
    main = np.zeros((2, 64, SPACE, 2, 4))
    for c in range(2):
        main[c, :, :, c, :] = both.reshape(64, SPACE, 4)
    main = main.reshape(128, 512)
    main2 = main.reshape(-1, SPACE, 2, 2, 2).transpose(0, 3, 1, 2, 4).reshape(-1, 512)
    both2 = both.reshape(-1, SPACE, 2, 2).transpose(0, 2, 1, 3).reshape(-1, 256)
    return [np.concatenate(halves(table), 0) for table in (main, main2, both, both2)]


def time_tables():
    def phase(q, step):
        return np.exp(-1j * angle(q if q < 8 else q - 16, step, NT))

    def pack(table, pad):
        high, low = halves(table)
        blank = np.zeros(table.shape[:-1] + (pad,), ml_dtypes.bfloat16)
        return np.concatenate([np.concatenate([part, part, blank], -1) for part in (high, low)], -2)

    out = []
    for count in (4, 2):
        table = np.zeros((2, 2, 2, 2, TM, 8, TM, 2, count, 4))
        for n in range(count):
            half, rest = divmod(n, count // 2)
            for q in range(16):
                for step in range(16):
                    value = phase(q, step)
                    for sx, sign in ((0, 1), (1, -1)):
                        at = (sx, q // 4, (q % 4) * 2 + rest, step // 4)
                        for zero in range(2):
                            if zero:
                                terms = ((sx, value),)
                            else:
                                terms = ((0, value), (1, -1j * sign * value))
                            for c, term in terms:
                                table[(zero, half, 0) + at + (c, n, step % 4)] = term.real
                                table[(zero, half, 1) + at + (c, n, step % 4)] = term.imag
        out.append(pack(table.reshape(2, 256, 32 * count), 0))
    table = np.zeros((3, 2, 2, TM, 8, TM, CH, 4))
    for n in range(CH):
        ng = n // 4
        half, rest = divmod(n % 4, 2) if ng < 2 else (n - 8, 0)
        for q in range(16):
            for step in range(16):
                term = 1j * phase(q, step)
                at = (q // 4, (q % 4) * 2 + rest, step // 4, n, step % 4)
                table[(ng, half, 0) + at] = term.real
                table[(ng, half, 1) + at] = term.imag
    out.append(pack(table.reshape(384, 160), 64))
    return out


def lane_tables():
    scale = 1.0 / math.sqrt(NX * NY * NZ * NT)
    out = np.zeros((3, 2, 2, 128, 2, 2, 2, 32))
    for sy, sign in ((0, 1), (1, -1)):
        for k in range(32):
            for kind in range(3):
                coef = np.zeros(128, complex)
                if kind == 0:
                    coef[k], coef[32 + k] = 1, -1j
                    coef[64 + k], coef[96 + k] = -1j * sign, -sign
                elif kind == 1:
                    at = 64 * sy
                    coef[at + k], coef[at + 32 + k] = 1, -1j
                elif sy == 1:
                    coef[k], coef[32 + k] = 1j, 1
                for w in range(2):
                    out[kind, w, 0, :, sy, w, 0, k] = coef.real
                    out[kind, w, 1, :, sy, w, 0, k] = -coef.imag
                    out[kind, w, 0, :, sy, w, 1, k] = coef.imag
                    out[kind, w, 1, :, sy, w, 1, k] = coef.real
    return (out.reshape(3, 512, 256) * scale).astype(ml_dtypes.bfloat16)


def all_tables():
    wx, wy = plane_tables()
    wz, wz2, wzb, wzb2 = depth_tables()
    m01, m2, mx = time_tables()
    pieces = {
        "wx": wx, "wy": wy.reshape(160, 256), "m01": m01.reshape(1024, 256), "m2": np.concatenate([m2[0], m2[1]], 1),
        "lanes": lane_tables().reshape(1536, 256), "wzb": wzb, "wzb2": wzb2,
    }
    for name, table in (("wz", wz), ("wz2", wz2), ("mx", mx)):
        wide = np.concatenate([table, np.zeros((len(table), -table.shape[1] % 256), ml_dtypes.bfloat16)], 1)
        pieces[name] = np.concatenate([wide[:, :256], wide[:, 256:]], 0)
    first, at = {}, 0
    for name, table in pieces.items():
        first[name] = at
        at += len(table)
    return np.concatenate(list(pieces.values()), 0), first


def split(values):
    high = values.astype(BF)
    return high, (values - high.astype(F32)).astype(BF)


def split_wide(values):
    scaled = values * 65537.0
    high = scaled - (scaled - values)
    return high, values - high


def dot(a, b):
    return jnp.dot(a, b, preferred_element_type=F32)


def owner(g, u):
    return jnp.where(u < 2, 2 * g + u, jnp.where(g == 0, 32, 64 - 2 * g) + u - 2)


def place(s):
    b, h = s // 2, s % 2
    g = jnp.where(b < 16, b, jnp.where(b == 16, 0, 32 - b))
    return g, jnp.where(b < 16, h, 2 + h)


def kernel(
    at_of, field, tables, out,
    planes, rows, rows_x, wx, wy, wz, wz2, wzb, wzb2, m01, m2, mx, lanes, lanes_b,
    send_a, send_b, recv_a, recv_b, time_send, time_send_x, time_sb, time_sbx,
    time_recv, time_recv_x, time_rb, time_rbx, sorts, last, blocks,
    field_sem, const_sem, ssa, rsa, ssx, rsx, ssb, rsb, sst, rst, sstx, rstx, sstb, rstb, sstbx, rstbx, ssl, rsl,
):
    s, tm = lax.axis_index("space"), lax.axis_index("tm")
    g, u = place(s)
    e = 4 * u + tm
    zero_g, zero_e, zero_u = g == 0, e == 0, u == 0
    pick_e, pick_g = jnp.where(zero_e, 1, 0), jnp.where(zero_g, 1, 0)

    def field_copy(pair):
        two = pl.ds(2 * pair, 2)
        return pltpu.make_async_copy(field.at[two], planes.at[two], field_sem.at[pair])

    def table_copy(i, dst, name, skip=0, columns=slice(None)):
        rows_at = pl.ds(pl.multiple_of(at_of[name] + skip, 16), dst.shape[0])
        return pltpu.make_async_copy(tables.at[rows_at, columns], dst, const_sem.at[i])

    consts = [
        table_copy(0, wx, "wx"),
        table_copy(1, wy, "wy"),
        table_copy(2, wz.at[:, :256], "wz"),
        table_copy(3, wz.at[:, 256:], "wz", 256),
        table_copy(4, wzb, "wzb"),
        table_copy(5, wzb2, "wzb2"),
        table_copy(6, m01, "m01", 512 * pick_e),
        table_copy(7, m2, "m2", 0, pl.ds(pl.multiple_of(128 * pick_e, 128), 128)),
        table_copy(8, mx.at[:, :256], "mx"),
        table_copy(9, mx.at[:, 256:], "mx", 768, slice(0, 128)),
        table_copy(10, lanes, "lanes", 512 * pick_g),
        table_copy(11, lanes_b, "lanes", 1024),
        table_copy(12, wz2.at[:, :256], "wz2"),
        table_copy(13, wz2.at[:, 256:], "wz2", 256),
    ]
    consts[0].start()
    field_copy(0).start()
    consts[1].start()

    barrier = pltpu.get_barrier_semaphore()

    def greet(space, time):
        pl.semaphore_signal(barrier, inc=1, device_id={"space": space, "tm": time}, device_id_type=MESH)


    def turn(value, count):
        return jnp.where(value >= count, value - count, value)

    place_x, place_y, place_z = s // 32, (s // 8) % 4, s % 8
    along = (
        [32 * turn(place_x + d, 2) for d in range(2)],
        [8 * turn(place_y + d, 4) for d in range(4)],
        [turn(place_z + d, 8) for d in range(8)],
    )
    others = [along[0][x] + along[1][y] + along[2][z] for x, y, z in OFFSETS]
    for to in others:
        greet(to, tm)

    for j in range(1, TM):
        greet(s, turn(tm + j, TM))
        for v in range(1, 4):
            greet(owner(g, turn(u + v, 4)), turn(tm + j, TM))

    for pair in range(1, CH // 2):
        field_copy(pair).start()
    for copy in consts[2:]:
        copy.start()

    rows_x[...] = jnp.zeros_like(rows_x)
    send_b[...] = jnp.zeros_like(send_b)

    def plane_step(ng, first, n):
        wx_wide = wx[...].astype(F32)
        products = []
        for t in range(4):
            for pair in range(2):
                high, low = split_wide(jnp.concatenate([planes[n, t, 2 * pair], planes[n, t, 2 * pair + 1]], axis=1))
                both = dot(wx_wide, jnp.concatenate([high, low], axis=0))
                products.append((t, pair, both[:40] + both[40:]))
        for t, pair, both in products:
            at = pl.multiple_of(((n - first) * 4 + t) * 8, 8)
            for half in range(2):
                z = 2 * pair + half
                part = both[:, 128 * half : 128 * half + 128]
                for v in range(4):
                    tile = part[8 * v : 8 * v + 8]
                    if ng < 2:
                        rows[ng, z, pl.ds(v * 128 + at, 8), :] = tile
                    else:
                        rows[2, half, pl.ds(v * 128 + pair * 64 + at, 8), :] = tile
                rows_x[half, pl.ds(64 * pair + 4 * n + t, 1), :] = part[32:33]

    def along_y(values, side):
        high, low = split(values)
        both = lax.dot_general(
            wy[80 * side : 80 * side + 80, :], jnp.concatenate([high, low], axis=1), (((1,), (1,)), ((), ())),
            preferred_element_type=F32,
        )
        return both[:40] + both[40:]

    def exchange(ng):
        count = 4 if ng < 2 else 2
        products = [
            (z, side, along_y(rows[ng, z, 256 * side : 256 * side + 256, :], side)) for z in range(count) for side in range(2)
        ]
        extras = [along_y(rows_x[z], 0) for z in range(2)] if ng == 2 else []
        for z, side, both in products:
            for h in range(2):
                lanes_h = slice(128 * h, 128 * h + 128)
                for c in range(2):
                    at = (side * 32 + h) * STEP + 8 * ng + count * c + z
                    send_a[pl.ds(at, 16, stride=2 * STEP), :] = both[16 * c : 16 * c + 16, lanes_h]
                send_b[pl.ds((2 * side + h) * 12 + 4 * ng + z, 1), :] = both[32:33, lanes_h]
        for z, both in enumerate(extras):
            for c in range(2):
                send_a[pl.ds(20 + 2 * c + z, 16, stride=2 * STEP), :] = both[16 * c : 16 * c + 16]
            send_b[pl.ds(10 + z, 1), :] = both[32:33]

    def sent(move):
        first, end = MOVES[move]
        return 8 * first, 8 * (end - first) - (4 if end == 3 else 0)

    def sent_b(move):
        first, end = MOVES[move]
        return 4 * first, 4 * (end - first)

    def remote(src, dst, send_sem, recv_sem, space, time):
        return pltpu.make_async_remote_copy(
            src_ref=src, dst_ref=dst, send_sem=send_sem, recv_sem=recv_sem,
            device_id={"space": space, "tm": time}, device_id_type=MESH,
        )

    def space_copy(move, to):
        first, count = sent(move)
        src = pl.ds(pl.multiple_of(to * STEP + first, 8), count)
        return remote(send_a.at[src], recv_a.at[s, pl.ds(first, count)], ssa.at[move], rsa.at[move], to, tm)

    def send_space(move):
        first, count = sent(move)
        here = (s, pl.ds(first, count))
        last_move = move == len(MOVES) - 1

        for to in others:
            space_copy(move, to).start()

        if last_move:
            here_x = (s, pl.ds(20, 4))

            @pl.loop(0, 16)
            def _(k):
                @pl.when(2 * k != s)
                def _():
                    src = pl.ds(pl.multiple_of(2 * k * STEP + 20, 4), 4)
                    remote(send_a.at[src], recv_a.at[here_x], ssx.at[0], rsx.at[0], 2 * k, tm).start()

            @pl.when(zero_u)
            def _():
                recv_a[here_x] = send_a[pl.ds(pl.multiple_of(s * STEP + 20, 4), 4), :]

        first_b, count_b = sent_b(move)
        here_b = (s, pl.ds(first_b, count_b))
        for v, to in enumerate((0, 1, 32, 33)):
            src = pl.ds(12 * v + first_b, count_b)

            @pl.when(s != to)
            def _():
                remote(send_b.at[src], recv_b.at[here_b], ssb.at[move], rsb.at[move], to, tm).start()

            @pl.when(s == to)
            def _():
                recv_b[here_b] = send_b[src, :]

        recv_a[here] = send_a[pl.ds(pl.multiple_of(s * STEP + first, 8), count), :]

    consts[0].wait()
    for ng, (first, count) in enumerate(GROUPS):
        @pl.loop(first, first + count, step=2)
        def _(n):
            field_copy(n // 2).wait()
            plane_step(ng, first, n)
            plane_step(ng, first, n + 1)

        if ng == 0:
            consts[1].wait()
        exchange(ng)
        if ng == 0:
            pl.semaphore_wait(barrier, 63 + 3 + 9)
        for move, (_, end) in enumerate(MOVES):
            if ng == end - 1:
                send_space(move)

    for copy in consts[2:]:
        copy.wait()

    def wait_rows(rows_of, count, sem):
        pltpu.make_async_copy(rows_of.at[pl.ds(0, count)], rows_of.at[pl.ds(0, count)], sem).wait()

    def moved(move):
        first, end = MOVES[move]
        return TIME_AT[first], TIME_AT[end] - TIME_AT[first]

    def keep_time(ng, sort, z_rows, src, src_x):
        count = (TIME_AT[ng + 1] - TIME_AT[ng]) // 2
        sort[...] = z_rows
        for v in range(TM):
            for c in range(2):
                at = 80 * v + TIME_AT[ng] + count * c
                src[at : at + count, :] = sort[pl.ds(2 * v + c, count, stride=8), :]
        if ng == 2:
            src_x[...] = z_rows[64:104]

    def send_time(move, src, src_x, dst, dst_x, send_sem, recv_sem, send_sem_x, recv_sem_x):
        first, count = moved(move)
        mine = pl.ds(pl.multiple_of(tm * 80 + first, 8), count)
        here = (tm, pl.ds(first, count))
        for j in range(1, TM):
            to = tm + j
            to = jnp.where(to >= TM, to - TM, to)
            there = pl.ds(pl.multiple_of(to * 80 + first, 8), count)
            remote(src.at[there], dst.at[here], send_sem.at[move], recv_sem.at[move], s, to).start()
        dst[here] = src[mine, :]
        if move == len(MOVES) - 1:
            at_x = pl.ds(pl.multiple_of(tm * 40, 8), 40)

            @pl.when(jnp.logical_and(zero_u, tm != 0))
            def _():
                remote(src_x, dst_x.at[at_x], send_sem_x.at[0], recv_sem_x.at[0], s, 0).start()

            @pl.when(zero_e)
            def _():
                dst_x[pl.ds(0, 40), :] = src_x[...]

    time_a = (time_send, time_send_x, time_recv, time_recv_x, sst, rst, sstx, rstx)
    time_b = (time_sb, time_sbx, time_rb, time_rbx, sstb, rstb, sstbx, rstbx)

    def received(ref, ng):
        size = ref.shape[1] // 3
        count = SPACE * size
        values = ref[:, size * ng : size * ng + size, :].reshape(count, 128) if ng < 2 else None
        if ng == 2:
            count //= 2
            main, extra = (
                ref[:, at : at + size // 2, :].reshape(count, 128) for at in (2 * size, 2 * size + size // 2)
            )
            lower = lax.broadcasted_iota(jnp.int32, (count, 128), 1) < 64
            values = jnp.concatenate(
                [jnp.where(lower, main, pltpu.roll(extra, 64, 1)), jnp.where(lower, pltpu.roll(main, 64, 1), extra)], axis=0
            )
        high, low = split(values)
        return jnp.concatenate([high, low], axis=1)

    def depth_step(move):
        first, end = MOVES[move]
        wait_rows(send_a, 63 * sent(move)[1], rsa.at[move])
        if end == 3:
            @pl.when(zero_u)
            def _():
                wait_rows(send_a, 63 * 4, rsx.at[0])

        z_rows = []
        for ng in range(first, end):
            both = dot(wz[...] if ng < 2 else wz2[...], received(recv_a, ng))
            z_rows.append((both[:128, :128] + both[:128, 128:] + both[128:, :128]).T)
        for ng in range(first, end):
            keep_time(ng, sorts.at[ng], z_rows[ng - first], *time_a[:2])
        send_time(move, *time_a)

        @pl.when(zero_g)
        def _():
            wait_rows(send_a, 63 * sent_b(move)[1], rsb.at[move])
            z_rows = []
            for ng in range(first, end):
                both = dot(wzb[...] if ng < 2 else wzb2[...], received(recv_b, ng))
                both = both[:64, :128] + both[:64, 128:] + both[64:, :128]
                z_rows.append(jnp.concatenate([both, jnp.zeros_like(both)], axis=0).T)
            for ng in range(first, end):
                keep_time(ng, sorts.at[3 + ng], z_rows[ng - first], *time_b[:2])
            send_time(move, *time_b)

    def finish(values, table, signs):
        high, low = split(values)
        fill = table.shape[1] - 2 * values.shape[0]
        parts = [high, low] + ([jnp.zeros((fill, 128), BF)] if fill else [])
        both = dot(table[...], jnp.concatenate(parts, axis=0))
        both = both[: both.shape[0] // 2] + both[both.shape[0] // 2 :]
        count = both.shape[0] // 4
        pairs = [split(both[count * i : count * i + count]) for i in range(4)]
        both = jnp.concatenate([jnp.concatenate([pair[i] for pair in pairs], axis=1) for i in range(2)], axis=0)
        both = dot(both, signs[...])
        return both[:count] + both[count:]

    def keep(ng, value, first, add, sides):
        for i in range(value.shape[0] // 8):
            for sy in sides:
                j = 8 * sy + first + i
                part = value[8 * i : 8 * i + 8, 128 * sy : 128 * sy + 128]
                at = slice(j * STEP + 8 * ng, j * STEP + 8 * ng + 8)
                last[at, :] = last[at, :] + part if add else part

    def slot_of(sx):
        return jnp.where(sx == 0, e, jnp.where(zero_e, 0, 16 - e))

    def last_copy(j, first, count):
        at = pl.ds(pl.multiple_of(slot_of((j // 4) % 2) * STEP + first, 8), count)
        src = pl.ds(pl.multiple_of(j * STEP + first, 8), count)
        return remote(last.at[src], blocks.at[at], ssl.at[0], rsl.at[0], owner(g, j // 4), j % 4)

    def steps_of(ref, ng):
        count = TIME_AT[ng + 1] - TIME_AT[ng]
        return ref[:, TIME_AT[ng] : TIME_AT[ng + 1], :].reshape(TM * count, 128)

    def time_step(move):
        first, end = MOVES[move]
        rows_at, rows_count = 8 * first, 8 * (end - first)

        def finish_all(ref, ref_x, signs, recv_sem_x, add, sides):
            values = [finish(steps_of(ref, ng), m01 if ng < 2 else m2, signs) for ng in range(first, end)]
            for ng in range(first, end):
                keep(ng, values[ng - first], 0, add, sides)
            if end == 3:
                @pl.when(zero_e)
                def _():
                    wait_rows(time_recv_x, 120, recv_sem_x.at[0])
                    value = finish_x(ref_x, signs)
                    for i in range(3):
                        keep(i, value[32 * i : 32 * i + 32], 4, True, sides)

        wait_rows(time_send, 3 * moved(move)[1], rst.at[move])
        finish_all(time_recv, time_recv_x, lanes, rstx, False, (0, 1))

        def send_side(side):
            @pl.when(jnp.logical_and(jnp.logical_not(zero_e), (e >= 8) == (side == 1)))
            def _():
                for k in range(1, 8):
                    last_copy(8 * side + turn(e - 8 * side + k, 8), rows_at, rows_count).start()

            @pl.when((e >= 8) != (side == 1))
            def _():
                for k in range(8):
                    if side == 0 or k < 4:
                        last_copy(8 * side + k, rows_at, rows_count).start()
                if side == 1:
                    @pl.when(jnp.logical_not(zero_e))
                    def _():
                        for k in range(4, 8):
                            last_copy(8 + k, rows_at, rows_count).start()

            @pl.when(zero_e)
            def _():
                if side == 0:
                    for j in range(1, 4):
                        last_copy(j, rows_at, rows_count).start()
                if end == 3:
                    for j in range(8 * side + 4, 8 * side + 8):
                        last_copy(j, 0, STEP).start()

        @pl.when(zero_g)
        def _():
            send_side(0)
            wait_rows(time_sb, 3 * moved(move)[1], rstb.at[move])
            finish_all(time_rb, time_rbx, lanes_b, rstbx, True, (1,))
            send_side(1)

        @pl.when(jnp.logical_and(jnp.logical_not(zero_g), e < 8))
        def _():
            send_side(1)
            send_side(0)

        @pl.when(jnp.logical_and(jnp.logical_not(zero_g), e >= 8))
        def _():
            send_side(0)
            send_side(1)

        at = pl.ds(pl.multiple_of(slot_of(u % 2) * STEP + rows_at, 8), rows_count)
        blocks[at, :] = last[pl.ds(pl.multiple_of(e * STEP + rows_at, 8), rows_count), :]

    def finish_x(ref, signs):
        high, low = split(ref[...])
        both = dot(mx[...], jnp.concatenate([high, low, jnp.zeros((64, 128), BF)], axis=0))
        both = both[:384] + both[384:]
        values = []
        for i in range(3):
            pairs = [split(both[128 * i + 32 * j : 128 * i + 32 * j + 32]) for j in range(4)]
            value = jnp.concatenate([jnp.concatenate([pair[h] for pair in pairs], axis=1) for h in range(2)], axis=0)
            value = dot(value, signs[...])
            values.append(value[:32] + value[32:])
        return jnp.concatenate(values, axis=0)

    for move in range(len(MOVES)):
        depth_step(move)
        time_step(move)

    wait_rows(blocks, 15 * STEP, rsl.at[0])
    for ng in range(3):
        for r in range(8):
            q, rest = r // 2, r % 2
            if ng == 2 and rest:
                continue
            value = blocks[pl.ds(8 * ng + r, 16, stride=STEP), :]
            for half in range(2):
                n = 4 * ng + 2 * half + rest if ng < 2 else 8 + half
                for part in range(2):
                    at = 64 * half + 32 * part
                    out[part, n, q] = value[:, at : at + 32]

    wait_rows(blocks, 15 * STEP, ssl.at[0])
    for move, (first, end) in enumerate(MOVES):
        wait_rows(send_a, 63 * sent(move)[1], ssa.at[move])

        @pl.when(zero_g)
        def _():
            wait_rows(send_b, 3 * sent_b(move)[1], ssb.at[move])

        @pl.when(jnp.logical_not(zero_g))
        def _():
            wait_rows(send_b, 4 * sent_b(move)[1], ssb.at[move])

    for move in range(len(MOVES)):
        wait_rows(time_send, 3 * moved(move)[1], sst.at[move])

        @pl.when(zero_g)
        def _():
            wait_rows(time_sb, 3 * moved(move)[1], sstb.at[move])

    @pl.when(zero_u)
    def _():
        wait_rows(send_a, 15 * 4, ssx.at[0])

    @pl.when(jnp.logical_not(zero_u))
    def _():
        wait_rows(send_a, 16 * 4, ssx.at[0])

    @pl.when(jnp.logical_and(zero_u, tm != 0))
    def _():
        wait_rows(time_send_x, 40, sstx.at[0])

        @pl.when(zero_g)
        def _():
            wait_rows(time_sbx, 40, sstbx.at[0])


def body(field):
    tables, at_of = all_tables()
    dma = pltpu.SemaphoreType.DMA

    def vmem(*shape):
        return pltpu.VMEM(shape, F32)

    def table(*shape):
        return pltpu.VMEM(shape, BF)

    return pl.pallas_call(
        functools.partial(kernel, at_of),
        out_shape=jax.ShapeDtypeStruct((2, CH, 4, 16, 32), F32),
        in_specs=[pl.BlockSpec(memory_space=pltpu.HBM)] * 2,
        out_specs=pl.BlockSpec(memory_space=pltpu.VMEM),
        scratch_shapes=[
            vmem(CH, 4, 4, 128, 128),
            vmem(3, 4, 512, 128), vmem(2, 128, 128),
            table(80, 256), table(160, 256), table(256, 512), table(256, 512), table(128, 256), table(128, 256),
            table(512, 256), table(512, 128), table(768, 384),
            table(512, 256), table(512, 256),
            vmem(64 * STEP, 128), vmem(48, 128), vmem(64, STEP, 128), vmem(64, 12, 128),
            vmem(320, 128), vmem(40, 128), vmem(320, 128), vmem(40, 128),
            vmem(4, 80, 128), vmem(160, 128), vmem(4, 80, 128), vmem(160, 128),
            vmem(6, 128, 128), vmem(16 * STEP, 128), vmem(16 * STEP, 128),
            dma((CH // 2,)), dma((14,)),
            dma((len(MOVES),)), dma((len(MOVES),)), dma((1,)), dma((1,)), dma((len(MOVES),)), dma((len(MOVES),)),
            dma((len(MOVES),)), dma((len(MOVES),)), dma((1,)), dma((1,)),
            dma((len(MOVES),)), dma((len(MOVES),)), dma((1,)), dma((1,)),
            dma((1,)), dma((1,)),
        ],
        compiler_params=pltpu.CompilerParams(
            collective_id=0, has_side_effects=True, vmem_limit_bytes=52 * 1024 * 1024
        ),
        cost_estimate=pl.CostEstimate(flops=20_000_000_000, bytes_accessed=13_000_000, transcendentals=0),
    )(field, tables)


def solution(mesh):
    return jax.shard_map(
        body,
        mesh=mesh,
        in_specs=(P(None, "tm", "space", None, None),),
        out_specs=P(None, None, "tm", "space", None),
        check_vma=False,
    )
```
